32 devices in a mesh: tm: 4 (over x, core), rows: 8 (over z, y).
Axes of the slice: x: 2, y: 2, z: 4, core: 2. Of those that a mesh axis runs over, the one named last changes fastest.
Arguments:
- video: bfloat16 [8, 16, 128, 128], P('tm', 'rows'), may hold values from -6 to 6
- kernel: bfloat16 [3, 3, 3, 128, 128], replicated, may hold values from -0.109375 to 0.109375
- cotangent: bfloat16 [8, 16, 128, 128], P('tm', 'rows'), may hold values from -6 to 6
Outputs:
- activated: bfloat16 [8, 16, 128, 128], P('tm', 'rows')
- input_grad: bfloat16 [8, 16, 128, 128], P('tm', 'rows')
- kernel_grad: float32 [128, 3456], P('rows', 'tm')
The draws below stay inside these ranges and needn't reach their ends.
All inputs are finite; a program needn't handle non-finite values.
Results may differ from the reference program's by a relative error of at most 0.0049.
Values may be sent and summed in bfloat16 or wider, within the bound.
A program may use at most 64 MiB of HBM per device.

```python
import jax
import jax.numpy as jnp
from jax import lax

C = 128
W = 128
FRAMES = 8
H = 16


def raised(drawn, stream_key, source, target, blocks, factor):
    def block_of(dim):
        return (jnp.arange(drawn.shape[dim]) // (drawn.shape[dim] // blocks)).reshape((-1,) + (1,) * (drawn.ndim - 1 - dim))

    near = jax.random.permutation(stream_key, blocks)[block_of(target)]
    other_side = (block_of(target) + blocks // 2) % blocks
    return jnp.where((block_of(source) == near) | (block_of(source) == other_side), factor * drawn, drawn)


def levels(stream_key, shape, shards, least, top_value):
    factor_of = 1.0
    for axis_at, parts in shards:
        heights = jax.random.uniform(jax.random.fold_in(jax.random.fold_in(stream_key, 6), axis_at), (parts,), jnp.float32, least / len(shards), top_value / len(shards))
        factor_of = factor_of * jnp.repeat(jnp.exp(heights), shape[axis_at] // parts).reshape((-1,) + (1,) * (len(shape) - 1 - axis_at))
    return factor_of


def noise(own_key, shape, scale, most, cuts=(), dtype=jnp.bfloat16):
    drawn = scale * jax.random.normal(own_key, shape, jnp.float32)
    if cuts:
        drawn = drawn * levels(own_key, shape, cuts, -0.22, 0.18)
    return jnp.clip(drawn, -most, most).astype(dtype)


def gaussian_with(stream_key, dims, scale, bound, split, heavy, kind=jnp.bfloat16):
    result = scale * jax.random.normal(stream_key, dims, jnp.float32)
    if split:
        result = result * levels(stream_key, dims, split, -0.22, 0.18)
    return jnp.clip(raised(result, jax.random.fold_in(stream_key, 3), *heavy), -bound, bound).astype(kind)


def setup_inputs(seed: int = 0) -> dict:
    key_list = jax.random.split(jax.random.key(seed), 4)
    return {
        "video": noise(key_list[0], (FRAMES, H, W, C), 1.0, 6.0, ((0, 4), (1, 8))),
        "kernel": noise(key_list[1], (3, 3, 3, C, C), (27 * C) ** -0.5, 0.109375),
        "cotangent": gaussian_with(key_list[2], (FRAMES, H, W, C), 1.0, 6.0, ((0, 4), (1, 8)), (1, 3, 8, 2.0)),
    }


def conv3(padded, kmat):
    lhs = padded.astype(jnp.float32)[None]
    rhs = kmat.astype(jnp.float32)
    out = lax.conv_general_dilated(lhs, rhs, (1, 1, 1), "VALID", dimension_numbers=("NDHWC", "DHWIO", "NDHWC"), precision=lax.Precision.HIGHEST)
    return out[0]


def reference(video, kernel, cotangent):
    padded = jnp.pad(video, ((2, 0), (1, 1), (1, 1), (0, 0)))
    pre = conv3(padded, kernel)
    sig = 1.0 / (1.0 + jnp.exp(-pre))
    activated = (pre * sig).astype(jnp.bfloat16)
    pre_grad = (cotangent.astype(jnp.float32) * sig * (1.0 + pre * (1.0 - sig))).astype(jnp.bfloat16)
    grad_padded = jnp.pad(pre_grad, ((0, 2), (1, 1), (1, 1), (0, 0)))
    flipped = jnp.transpose(kernel[::-1, ::-1, ::-1], (0, 1, 2, 4, 3))
    input_grad = conv3(grad_padded, flipped).astype(jnp.bfloat16)
    grad_float = pre_grad.astype(jnp.float32)
    padded_float = padded.astype(jnp.float32)
    blocks = []
    for a in range(3):
        for b in range(3):
            for c in range(3):
                window = padded_float[a:a + FRAMES, b:b + H, c:c + W]
                blocks.append(jnp.einsum("thwi,thwo->oi", window, grad_float, precision=lax.Precision.HIGHEST))
    kernel_grad = jnp.concatenate(blocks, axis=1)
    return activated, input_grad, kernel_grad
```

```python
import functools

import jax
import jax.numpy as jnp
from jax import lax
from jax.experimental import pallas as pl
from jax.experimental.pallas import tpu as pltpu
from jax.sharding import PartitionSpec as P

MESH = pl.DeviceIdType.MESH
F32 = jnp.float32
BF16 = jnp.bfloat16


def along_width(lines, width):
    count, _, chans = lines.shape
    flat = lines.reshape(count * width, chans).astype(F32)
    column = lax.broadcasted_iota(jnp.int32, (count, width, chans), 1).reshape(flat.shape)
    before = jnp.where(column == 0, 0.0, pltpu.roll(flat, 1, 0)).astype(BF16)
    after = jnp.where(column == width - 1, 0.0, pltpu.roll(flat, count * width - 1, 0)).astype(BF16)
    return (
        before.reshape(lines.shape),
        lines,
        after.reshape(lines.shape),
    )


def kernel(
    nt, nr, reduce_here,
    video, weights, cot, act, igrad, kgrad,
    taps, seen, patches, gext, gpatches, total, chunks,
    s0, r0, a1, s1a, r1a, s1b, r1b, a2a, a2b, s2a, r2a, s2b, r2b, a3, s3, r3,
    local_sem, vsend, vrecv, gsend, grecv, ksend, krecv,
):
    frames, height, width, chans = video.shape
    rows = frames * height * width
    tm = lax.axis_index("tm")
    row = lax.axis_index("rows")

    def inside(dt, dr):
        return (tm + dt >= 0) & (tm + dt < nt) & (row + dr >= 0) & (row + dr < nr)

    def wrapped(dt, dr):
        return (lax.rem(tm + dt + nt, nt), lax.rem(row + dr + nr, nr))

    load = pltpu.make_async_copy(weights, taps, local_sem)
    load.start()

    barrier = pltpu.get_barrier_semaphore()
    around = [(dt, dr) for dt in (-1, 0, 1) for dr in (-1, 0, 1) if dt or dr]
    expected = 0
    for dt, dr in around:
        there = inside(dt, dr)
        expected = expected + jnp.where(there, 1, 0)

        @pl.when(there)
        def _(dt=dt, dr=dr):
            pl.semaphore_signal(barrier, inc=1, device_id=wrapped(dt, dr), device_id_type=MESH)

    if reduce_here:
        depth = lax.div(row, 2)
        side = lax.rem(row, 2)
        across = lax.div(tm, 2)
        core = lax.rem(tm, 2)
        other_core = (across * 2 + 1 - core, row)
        other_across = ((1 - across) * 2 + core, row)
        other_side = (tm, depth * 2 + 1 - side)
        layers = [lax.rem(depth + k, 4) for k in range(4)]
        partners = [other_across] + [(tm, layers[k] * 2 + side) for k in (1, 2, 3)]
        for partner in partners:
            pl.semaphore_signal(barrier, inc=1, device_id=partner, device_id_type=MESH)
        expected = expected + len(partners)
    pl.semaphore_wait(barrier, expected)

    def exchange(pieces, send_sems, recv_sems):
        copies = []
        for k, (dt, dr, source, target) in enumerate(pieces):
            copy = pltpu.make_async_remote_copy(
                src_ref=source, dst_ref=target,
                send_sem=send_sems.at[k], recv_sem=recv_sems.at[k],
                device_id=wrapped(dt, dr), device_id_type=MESH,
            )
            copies.append(copy)
            pl.when(inside(dt, dr))(copy.start)

        def arrive(k):
            dt, dr, _, target = pieces[k]
            there = inside(-dt, -dr)
            pl.when(there)(copies[k].wait_recv)

            @pl.when(jnp.logical_not(there))
            def _():
                target[...] = jnp.zeros(target.shape, BF16)

        def finish():
            for k, (dt, dr, _, _) in enumerate(pieces):
                pl.when(inside(dt, dr))(copies[k].wait_send)

        return arrive, finish

    own, top, bottom = pl.ds(1, height), 0, height + 1
    old, new = pl.ds(0, 2), pl.ds(2, frames)
    last = pl.ds(frames - 2, 2)
    arrive_v, finish_v = exchange(
        [
            (1, 0, video.at[last], seen.at[old, own]),
            (0, 1, video.at[:, height - 1], seen.at[new, top]),
            (0, -1, video.at[:, 0], seen.at[new, bottom]),
            (1, 1, video.at[last, height - 1], seen.at[old, top]),
            (1, -1, video.at[last, 0], seen.at[old, bottom]),
        ],
        vsend, vrecv,
    )

    def spread(target, fr, ro, lines):
        flat = lines.reshape((-1,) + lines.shape[-2:])
        for c, piece in enumerate(along_width(flat, width)):
            target[fr, ro, :, c * chans:(c + 1) * chans] = piece.reshape(lines.shape)

    def patch(source, a, b):
        return source[a:a + frames, b:b + height].reshape(rows, 3 * chans)

    def forward(a, b):
        return jnp.dot(patch(patches, a, b), taps[a * 3 + b], preferred_element_type=F32)

    spread(patches, new, own, video[...])
    load.wait()
    pre = forward(2, 1)
    arrive_v(0)
    spread(patches, old, own, seen[old, own])
    pre = pre + forward(0, 1)
    pre = pre + forward(1, 1)
    for k, fr, ro in ((1, new, top), (2, new, bottom), (3, old, top), (4, old, bottom)):
        arrive_v(k)
        spread(patches, fr, ro, seen[fr, ro])
    for b in (0, 2):
        for a in range(3):
            pre = pre + forward(a, b)

    sig = 1.0 / (1.0 + jnp.exp(-pre))
    act[...] = (pre * sig).astype(BF16).reshape(act.shape)
    cot_flat = cot[...].reshape(rows, chans).astype(F32)
    grad = (cot_flat * sig * (1.0 + pre * (1.0 - sig))).astype(BF16)
    mine, later = pl.ds(0, frames), pl.ds(frames, 2)
    early = pl.ds(0, 2)
    gext[mine, own] = grad.reshape(video.shape)
    arrive_g, finish_g = exchange(
        [
            (-1, 0, gext.at[early, own], gext.at[later, own]),
            (0, 1, gext.at[mine, height], gext.at[mine, top]),
            (0, -1, gext.at[mine, 1], gext.at[mine, bottom]),
            (-1, 1, gext.at[early, height], gext.at[later, top]),
            (-1, -1, gext.at[early, 1], gext.at[later, bottom]),
        ],
        gsend, grecv,
    )

    turned = grad.astype(F32).T.astype(BF16)
    kdepth = 3 * chans

    def weight_part(k):
        total[:, k * kdepth:(k + 1) * kdepth] = jnp.dot(
            turned, patch(patches, k // 3, k % 3), preferred_element_type=F32
        )

    def backward(a, b):
        block = taps.at[(2 - a) * 3 + 2 - b]
        mat = jnp.concatenate(
            [block[(2 - c) * chans:(3 - c) * chans, :] for c in range(3)], axis=1
        )
        return lax.dot_general(
            patch(gpatches, a, b), mat, (((1,), (1,)), ((), ())), preferred_element_type=F32
        )

    def grad_own():
        spread(gpatches, mine, own, grad.reshape(video.shape))
        return backward(0, 1)

    def grad_later(out):
        arrive_g(0)
        spread(gpatches, later, own, gext[later, own])
        return out + backward(1, 1) + backward(2, 1)

    def grad_edges():
        for k, fr, ro in ((1, mine, top), (2, mine, bottom), (3, later, top), (4, later, bottom)):
            arrive_g(k)
            spread(gpatches, fr, ro, gext[fr, ro])

    if not reduce_here:
        for k in range(9):
            weight_part(k)
        kgrad[...] = total[...]
        out = grad_later(grad_own())
        grad_edges()
        for b in (0, 2):
            for a in range(3):
                out = out + backward(a, b)
        igrad[...] = out.astype(BF16).reshape(igrad.shape)
        finish_v()
        finish_g()
        return

    columns = total.shape[1] // nt
    wide = chunks.shape[-1]

    def cut(j):
        start = columns * j // 128 * 128
        shift = columns * j - start
        span = -(-(shift + columns) // 128) * 128
        piece = total[:, start:start + span]
        if shift:
            piece = pltpu.roll(piece, span - shift, 1)
        chunks[j] = piece[:, :wide].reshape(chunks.shape[1:])

    def send(k, source, target, device):
        copy = pltpu.make_async_remote_copy(
            src_ref=source, dst_ref=target,
            send_sem=ksend.at[k], recv_sem=krecv.at[k],
            device_id=device, device_id_type=MESH,
        )
        copy.start()
        return copy

    copies = []
    done = 0
    for half in range(2):
        need = -(-columns * (2 * half + 2) // kdepth)
        for k in range(done, need):
            weight_part(k)
        done = need
        cut(2 * half)
        cut(2 * half + 1)
        s0[half] = chunks[2 * half + 1 - core].astype(BF16)
        copies.append(send(half, s0.at[half], r0.at[half], other_core))

    out = grad_own()

    for half in range(2):
        copies[half].wait_recv()
        a1[half] = chunks[2 * half + core] + r0[half].astype(F32)
    s1a[...] = a1[1 - across, 0:2].astype(BF16)
    copies.append(send(2, s1a, r1a, other_across))
    s1b[...] = a1[:, 2:4, 1 - side].astype(BF16)
    copies.append(send(3, s1b, r1b, other_side))

    out = grad_later(out)
    grad_edges()

    copies[2].wait_recv()
    a2a[...] = a1[across, 0:2] + r1a[...].astype(F32)
    s2a[...] = a2a[:, 1 - side].astype(BF16)
    copies.append(send(4, s2a, r2a, other_side))
    copies[3].wait_recv()
    a2b[...] = a1[:, 2:4, side] + r1b[...].astype(F32)
    s2b[...] = a2b[1 - across].astype(BF16)
    copies.append(send(5, s2b, r2b, other_across))

    for a in range(3):
        out = out + backward(a, 0)

    copies[4].wait_recv()
    a3[0:2] = a2a[:, side] + r2a[...].astype(F32)
    copies[5].wait_recv()
    a3[2:4] = a2b[across] + r2b[...].astype(F32)
    for k in (1, 2, 3):
        s3[k - 1] = a3[layers[k]].astype(BF16)
        copies.append(
            send(5 + k, s3.at[k - 1], r3.at[k - 1], (tm, layers[k] * 2 + side))
        )

    for a in range(3):
        out = out + backward(a, 2)
    igrad[...] = out.astype(BF16).reshape(igrad.shape)

    owned = a3[depth]
    for k in (1, 2, 3):
        copies[5 + k].wait_recv()
        owned = owned + r3[k - 1].astype(F32)
    kgrad[...] = owned[:, :columns]
    for copy in copies:
        copy.wait_send()
    finish_v()
    finish_g()


def local(nt, nr, video, weights, cotangent):
    frames, height, width, chans = video.shape
    rows = frames * height * width
    cols = 27 * chans
    share, columns = chans // nr, cols // nt
    reduce_here = nt == 4 and nr == 8 and share % 16 == 0
    wide = -(-columns // 128) * 128 if reduce_here else 128
    sh = share if reduce_here else 16
    vm = pltpu.VMEM
    full = pl.BlockSpec(memory_space=pltpu.VMEM)
    scratch = [
        vm((9, 3 * chans, chans), BF16),
        vm((frames + 2, height + 2, width, chans), BF16),
        vm((frames + 2, height + 2, width, 3 * chans), BF16),
        vm((frames + 2, height + 2, width, chans), BF16),
        vm((frames + 2, height + 2, width, 3 * chans), BF16),
        vm((chans, cols), F32),
        vm((4, 4, 2, sh, wide), F32),
        vm((2, 4, 2, sh, wide), BF16),
        vm((2, 4, 2, sh, wide), BF16),
        vm((2, 4, 2, sh, wide), F32),
        vm((2, 2, sh, wide), BF16),
        vm((2, 2, sh, wide), BF16),
        vm((2, 2, sh, wide), BF16),
        vm((2, 2, sh, wide), BF16),
        vm((2, 2, sh, wide), F32),
        vm((2, 2, sh, wide), F32),
        vm((2, sh, wide), BF16),
        vm((2, sh, wide), BF16),
        vm((2, sh, wide), BF16),
        vm((2, sh, wide), BF16),
        vm((4, sh, wide), F32),
        vm((3, sh, wide), BF16),
        vm((3, sh, wide), BF16),
        pltpu.SemaphoreType.DMA,
        pltpu.SemaphoreType.DMA((5,)),
        pltpu.SemaphoreType.DMA((5,)),
        pltpu.SemaphoreType.DMA((5,)),
        pltpu.SemaphoreType.DMA((5,)),
        pltpu.SemaphoreType.DMA((9,)),
        pltpu.SemaphoreType.DMA((9,)),
    ]
    kshape = (share, columns) if reduce_here else (chans, cols)
    activated, input_grad, kgrad = pl.pallas_call(
        functools.partial(kernel, nt, nr, reduce_here),
        out_shape=(
            jax.ShapeDtypeStruct(video.shape, BF16),
            jax.ShapeDtypeStruct(video.shape, BF16),
            jax.ShapeDtypeStruct(kshape, F32),
        ),
        in_specs=[full, pl.BlockSpec(memory_space=pl.ANY), full],
        out_specs=(full, full, full),
        scratch_shapes=scratch,
        compiler_params=pltpu.CompilerParams(
            collective_id=0, has_side_effects=True, vmem_limit_bytes=40 * 1024 * 1024
        ),
        cost_estimate=pl.CostEstimate(
            flops=6 * rows * cols * chans, bytes_accessed=4 * 1024 * 1024, transcendentals=rows * chans
        ),
        name="conv_silu_grads",
    )(video, weights.reshape(9, 3 * chans, chans), cotangent)
    if not reduce_here:
        kgrad = lax.psum_scatter(kgrad, "rows", scatter_dimension=0, tiled=True)
        kgrad = lax.psum_scatter(kgrad, "tm", scatter_dimension=1, tiled=True)
    return activated, input_grad, kgrad


def solution(mesh):
    split = P("tm", "rows", None, None)
    return jax.shard_map(
        functools.partial(local, mesh.shape["tm"], mesh.shape["rows"]),
        mesh=mesh,
        in_specs=(split, P(), split),
        out_specs=(split, split, P("rows", "tm")),
        check_vma=False,
    )
```

```python
import functools

import jax
import jax.numpy as jnp
from jax import lax
from jax.experimental import pallas as pl
from jax.experimental.pallas import tpu as pltpu
from jax.sharding import PartitionSpec as P

MESH = pl.DeviceIdType.MESH
F32 = jnp.float32
BF16 = jnp.bfloat16
VMEM_BYTES = 56 * 1024 * 1024


def along_width(lines, width):
    count, _, chans = lines.shape
    flat = lines.reshape(count * width, chans).astype(F32)
    column = lax.broadcasted_iota(jnp.int32, (count, width, chans), 1).reshape(flat.shape)
    before = jnp.where(column == 0, 0.0, pltpu.roll(flat, 1, 0)).astype(BF16)
    after = jnp.where(column == width - 1, 0.0, pltpu.roll(flat, count * width - 1, 0)).astype(BF16)
    return (
        before.reshape(lines.shape),
        lines,
        after.reshape(lines.shape),
    )


def kernel(
    nt, nr, reduce_here,
    video, weights, cot, act_out, igrad_out, kgrad_out,
    act, igrad, kgrad, taps, cot_own, seen, patches, gext, gpatches, total, chunks,
    s0, r0, a1, s1a, r1a, s1b, r1b, a2a, a2b, s2a, r2a, s2b, r2b, a3, s3, r3,
    local_sem, vsend, vrecv, gsend, grecv, ksend, krecv,
):
    frames, height, width, chans = video.shape
    rows = frames * height * width
    tm = lax.axis_index("tm")
    row = lax.axis_index("rows")

    def inside(dt, dr):
        return (tm + dt >= 0) & (tm + dt < nt) & (row + dr >= 0) & (row + dr < nr)

    def wrapped(dt, dr):
        return (lax.rem(tm + dt + nt, nt), lax.rem(row + dr + nr, nr))

    own, top, bottom = pl.ds(1, height), 0, height + 1
    old, new = pl.ds(0, 2), pl.ds(2, frames)
    loads = [
        pltpu.make_async_copy(video, seen.at[new, own], local_sem.at[0]),
        pltpu.make_async_copy(weights, taps, local_sem.at[1]),
        pltpu.make_async_copy(cot, cot_own, local_sem.at[2]),
    ]
    for load in loads:
        load.start()

    barrier = pltpu.get_barrier_semaphore()
    odd = lax.rem(tm, 2) == 1
    around = [(dt, dr) for dt in (-1, 0, 1) for dr in (-1, 0, 1) if dt or dr]
    expected = 0
    for dt, dr in around:
        greets = copies_to = inside(dt, dr)
        if dt and dr:
            greets = greets & (dt == -1) & jnp.logical_not(odd)
            copies_to = copies_to & (dt == 1) & odd
        expected = expected + jnp.where(copies_to, 1, 0)

        @pl.when(greets)
        def _(dt=dt, dr=dr):
            pl.semaphore_signal(barrier, inc=1, device_id=wrapped(dt, dr), device_id_type=MESH)

    if reduce_here:
        depth = lax.div(row, 2)
        side = lax.rem(row, 2)
        across = lax.div(tm, 2)
        core = lax.rem(tm, 2)
        other_core = (across * 2 + 1 - core, row)
        other_across = ((1 - across) * 2 + core, row)
        other_side = (tm, depth * 2 + 1 - side)
        layers = [lax.rem(depth + k, 4) for k in range(4)]
        partners = [other_across] + [(tm, layers[k] * 2 + side) for k in (1, 2, 3)]
        for partner in partners:
            pl.semaphore_signal(barrier, inc=1, device_id=partner, device_id_type=MESH)
        expected = expected + len(partners)
    pl.semaphore_wait(barrier, expected)

    def piece(dt, dr, send_when, source, target, sems, k):
        copy = pltpu.make_async_remote_copy(
            src_ref=source, dst_ref=target,
            send_sem=sems[0].at[k], recv_sem=sems[1].at[k],
            device_id=wrapped(dt, dr), device_id_type=MESH,
        )
        return (copy, send_when)

    def start(part):
        pl.when(part[1])(part[0].start)

    def sent(part):
        pl.when(part[1])(part[0].wait_send)

    def arrive(part, dt, dr, target):
        there = inside(dt, dr)
        pl.when(there)(part[0].wait_recv)

        @pl.when(jnp.logical_not(there))
        def _():
            target[...] = jnp.zeros(target.shape, BF16)

    last = pl.ds(frames - 2, 2)
    vsems, gsems = (vsend, vrecv), (gsend, grecv)
    halo = [
        piece(1, 0, inside(1, 0), video.at[last], seen.at[old, own], vsems, 0),
        piece(0, 1, inside(0, 1), video.at[:, height - 1], seen.at[new, top], vsems, 1),
        piece(0, -1, inside(0, -1), video.at[:, 0], seen.at[new, bottom], vsems, 2),
        piece(1, 1, inside(1, 1) & odd, video.at[last, height - 1], seen.at[old, top], vsems, 3),
        piece(1, -1, inside(1, -1) & odd, video.at[last, 0], seen.at[old, bottom], vsems, 4),
    ]
    for part in halo:
        start(part)
    even = jnp.logical_not(odd)
    newest = pl.ds(frames, 2)
    passed = [
        piece(1, 0, inside(1, -1) & even, seen.at[newest, top], seen.at[old, top], vsems, 3),
        piece(1, 0, inside(1, 1) & even, seen.at[newest, bottom], seen.at[old, bottom], vsems, 4),
    ]

    def spread(target, fr, ro, lines):
        flat = lines.reshape((-1,) + lines.shape[-2:])
        for c, piece in enumerate(along_width(flat, width)):
            target[fr, ro, :, c * chans:(c + 1) * chans] = piece.reshape(lines.shape)

    def patch(source, a, b):
        return source[a:a + frames, b:b + height].reshape(rows, 3 * chans)

    def forward(a, b):
        return jnp.dot(patch(patches, a, b), taps[a * 3 + b], preferred_element_type=F32)

    loads[0].wait()
    spread(patches, new, own, seen[new, own])
    loads[1].wait()
    pre = forward(2, 1)
    arrive(halo[0], -1, 0, seen.at[old, own])
    spread(patches, old, own, seen[old, own])
    pre = pre + forward(0, 1)
    pre = pre + forward(1, 1)
    arrive(halo[1], 0, -1, seen.at[new, top])
    start(passed[0])
    arrive(halo[2], 0, 1, seen.at[new, bottom])
    start(passed[1])
    spread(patches, new, top, seen[new, top])
    spread(patches, new, bottom, seen[new, bottom])
    pre = pre + forward(2, 0)
    pre = pre + forward(2, 2)
    arrive(halo[3], -1, -1, seen.at[old, top])
    spread(patches, old, top, seen[old, top])
    arrive(halo[4], -1, 1, seen.at[old, bottom])
    spread(patches, old, bottom, seen[old, bottom])
    for b in (0, 2):
        for a in range(2):
            pre = pre + forward(a, b)

    sig = 1.0 / (1.0 + jnp.exp(-pre))
    act[...] = (pre * sig).astype(BF16).reshape(act.shape)
    loads[2].wait()
    stores = [
        pltpu.make_async_copy(act, act_out, local_sem.at[3]),
        pltpu.make_async_copy(igrad, igrad_out, local_sem.at[4]),
        pltpu.make_async_copy(kgrad, kgrad_out, local_sem.at[5]),
    ]
    stores[0].start()
    cot_flat = cot_own[...].reshape(rows, chans).astype(F32)
    grad = (cot_flat * sig * (1.0 + pre * (1.0 - sig))).astype(BF16)
    mine, later = pl.ds(0, frames), pl.ds(frames, 2)
    early = pl.ds(0, 2)
    gext[mine, own] = grad.reshape(video.shape)
    ghalo = [
        piece(-1, 0, inside(-1, 0), gext.at[early, own], gext.at[later, own], gsems, 0),
        piece(0, 1, inside(0, 1), gext.at[mine, height], gext.at[mine, top], gsems, 1),
        piece(0, -1, inside(0, -1), gext.at[mine, 1], gext.at[mine, bottom], gsems, 2),
        piece(-1, 0, inside(-1, -1), gext.at[early, top], gext.at[later, top], gsems, 3),
        piece(-1, 0, inside(-1, 1), gext.at[early, bottom], gext.at[later, bottom], gsems, 4),
    ]
    for part in ghalo[:3]:
        start(part)

    turned = grad.astype(F32).T.astype(BF16)
    kdepth = 3 * chans

    def weight_part(k):
        total[:, k * kdepth:(k + 1) * kdepth] = jnp.dot(
            turned, patch(patches, k // 3, k % 3), preferred_element_type=F32
        )

    def backward(a, b):
        block = taps.at[(2 - a) * 3 + 2 - b]
        mat = jnp.concatenate(
            [block[(2 - c) * chans:(3 - c) * chans, :] for c in range(3)], axis=1
        )
        return lax.dot_general(
            patch(gpatches, a, b), mat, (((1,), (1,)), ((), ())), preferred_element_type=F32
        )

    def grad_own():
        spread(gpatches, mine, own, grad.reshape(video.shape))
        return backward(0, 1)

    def grad_later(out):
        arrive(ghalo[0], 1, 0, gext.at[later, own])
        spread(gpatches, later, own, gext[later, own])
        return out + backward(1, 1) + backward(2, 1)

    def grad_rows():
        arrive(ghalo[1], 0, -1, gext.at[mine, top])
        start(ghalo[3])
        arrive(ghalo[2], 0, 1, gext.at[mine, bottom])
        start(ghalo[4])

    def grad_edges(out):
        for ro in (top, bottom):
            spread(gpatches, mine, ro, gext[mine, ro])
        return out + backward(0, 0) + backward(0, 2)

    def grad_corners(out):
        arrive(ghalo[3], 1, -1, gext.at[later, top])
        spread(gpatches, later, top, gext[later, top])
        out = out + backward(1, 0) + backward(2, 0)
        arrive(ghalo[4], 1, 1, gext.at[later, bottom])
        spread(gpatches, later, bottom, gext[later, bottom])
        out = out + backward(1, 2) + backward(2, 2)
        igrad[...] = out.astype(BF16).reshape(igrad.shape)
        stores[1].start()

    def finish():
        for part in halo + passed + ghalo:
            sent(part)
        for store in stores:
            store.wait()

    if not reduce_here:
        for k in range(9):
            weight_part(k)
        kgrad[...] = total[...]
        stores[2].start()
        out = grad_later(grad_own())
        grad_rows()
        grad_corners(grad_edges(out))
        finish()
        return

    columns = total.shape[1] // nt
    wide = chunks.shape[-1]

    def cut(j):
        start = columns * j // 128 * 128
        shift = columns * j - start
        span = -(-(shift + columns) // 128) * 128
        piece = total[:, start:start + span]
        if shift:
            piece = pltpu.roll(piece, span - shift, 1)
        chunks[j] = piece[:, :wide].reshape(chunks.shape[1:])

    def send(k, source, target, device):
        copy = pltpu.make_async_remote_copy(
            src_ref=source, dst_ref=target,
            send_sem=ksend.at[k], recv_sem=krecv.at[k],
            device_id=device, device_id_type=MESH,
        )
        copy.start()
        return copy

    copies = []
    done = 0
    for half in range(2):
        need = -(-columns * (2 * half + 2) // kdepth)
        for k in range(done, need):
            weight_part(k)
        done = need
        cut(2 * half)
        cut(2 * half + 1)
        s0[half] = chunks[2 * half + 1 - core].astype(BF16)
        copies.append(send(half, s0.at[half], r0.at[half], other_core))

    out = grad_own()

    for half in range(2):
        copies[half].wait_recv()
        a1[half] = chunks[2 * half + core] + r0[half].astype(F32)
    s1a[...] = a1[1 - across, 0:2].astype(BF16)
    copies.append(send(2, s1a, r1a, other_across))
    s1b[...] = a1[:, 2:4, 1 - side].astype(BF16)
    copies.append(send(3, s1b, r1b, other_side))

    out = grad_later(out)

    copies[2].wait_recv()
    a2a[...] = a1[across, 0:2] + r1a[...].astype(F32)
    s2a[...] = a2a[:, 1 - side].astype(BF16)
    copies.append(send(4, s2a, r2a, other_side))
    copies[3].wait_recv()
    a2b[...] = a1[:, 2:4, side] + r1b[...].astype(F32)
    s2b[...] = a2b[1 - across].astype(BF16)
    copies.append(send(5, s2b, r2b, other_across))

    grad_rows()
    out = grad_edges(out)

    copies[4].wait_recv()
    a3[0:2] = a2a[:, side] + r2a[...].astype(F32)
    copies[5].wait_recv()
    a3[2:4] = a2b[across] + r2b[...].astype(F32)
    for k in (1, 2, 3):
        s3[k - 1] = a3[layers[k]].astype(BF16)
        copies.append(
            send(5 + k, s3.at[k - 1], r3.at[k - 1], (tm, layers[k] * 2 + side))
        )

    grad_corners(out)

    owned = a3[depth]
    for k in (1, 2, 3):
        copies[5 + k].wait_recv()
        owned = owned + r3[k - 1].astype(F32)
    kgrad[...] = owned[:, :columns]
    stores[2].start()
    for copy in copies:
        copy.wait_send()
    finish()


def deliver(*refs):
    count = (len(refs) - 1) // 2
    copies = [pltpu.make_async_copy(refs[k], refs[count + k], refs[-1].at[k]) for k in range(count)]
    for copy in copies:
        copy.start()
    for copy in copies:
        copy.wait()


def local(nt, nr, video, weights, cotangent):
    frames, height, width, chans = video.shape
    rows = frames * height * width
    cols = 27 * chans
    share, columns = chans // nr, cols // nt
    reduce_here = nt == 4 and nr == 8 and share % 16 == 0
    wide = -(-columns // 128) * 128 if reduce_here else 128
    sh = share if reduce_here else 16
    vm = pltpu.VMEM
    far = pl.BlockSpec(memory_space=pl.ANY)
    kshape = (share, columns) if reduce_here else (chans, cols)
    scratch = [
        vm(video.shape, BF16),
        vm(video.shape, BF16),
        vm(kshape, F32),
        vm((9, 3 * chans, chans), BF16),
        vm(video.shape, BF16),
        vm((frames + 2, height + 2, width, chans), BF16),
        vm((frames + 2, height + 2, width, 3 * chans), BF16),
        vm((frames + 2, height + 2, width, chans), BF16),
        vm((frames + 2, height + 2, width, 3 * chans), BF16),
        vm((chans, cols), F32),
        vm((4, 4, 2, sh, wide), F32),
        vm((2, 4, 2, sh, wide), BF16),
        vm((2, 4, 2, sh, wide), BF16),
        vm((2, 4, 2, sh, wide), F32),
        vm((2, 2, sh, wide), BF16),
        vm((2, 2, sh, wide), BF16),
        vm((2, 2, sh, wide), BF16),
        vm((2, 2, sh, wide), BF16),
        vm((2, 2, sh, wide), F32),
        vm((2, 2, sh, wide), F32),
        vm((2, sh, wide), BF16),
        vm((2, sh, wide), BF16),
        vm((2, sh, wide), BF16),
        vm((2, sh, wide), BF16),
        vm((4, sh, wide), F32),
        vm((3, sh, wide), BF16),
        vm((3, sh, wide), BF16),
        pltpu.SemaphoreType.DMA((6,)),
        pltpu.SemaphoreType.DMA((5,)),
        pltpu.SemaphoreType.DMA((5,)),
        pltpu.SemaphoreType.DMA((5,)),
        pltpu.SemaphoreType.DMA((5,)),
        pltpu.SemaphoreType.DMA((9,)),
        pltpu.SemaphoreType.DMA((9,)),
    ]
    activated, input_grad, kgrad = pl.pallas_call(
        functools.partial(kernel, nt, nr, reduce_here),
        out_shape=(
            jax.ShapeDtypeStruct(video.shape, BF16),
            jax.ShapeDtypeStruct(video.shape, BF16),
            jax.ShapeDtypeStruct(kshape, F32),
        ),
        in_specs=[far, far, far],
        out_specs=(far, far, far),
        scratch_shapes=scratch,
        compiler_params=pltpu.CompilerParams(
            collective_id=0, has_side_effects=True, vmem_limit_bytes=VMEM_BYTES
        ),
        cost_estimate=pl.CostEstimate(
            flops=6 * rows * cols * chans, bytes_accessed=4 * 1024 * 1024, transcendentals=rows * chans
        ),
        name="conv_silu_grads",
    )(video, weights.reshape(9, 3 * chans, chans), cotangent)
    if not reduce_here:
        kgrad = lax.psum_scatter(kgrad, "rows", scatter_dimension=0, tiled=True)
        kgrad = lax.psum_scatter(kgrad, "tm", scatter_dimension=1, tiled=True)
        return activated, input_grad, kgrad
    results = (activated, input_grad, kgrad)
    return pl.pallas_call(
        deliver,
        out_shape=tuple(jax.ShapeDtypeStruct(x.shape, x.dtype) for x in results),
        in_specs=[far] * 3,
        out_specs=(far,) * 3,
        scratch_shapes=[pltpu.SemaphoreType.DMA((3,))],
        compiler_params=pltpu.CompilerParams(vmem_limit_bytes=VMEM_BYTES),
        name="deliver",
    )(*results)


def solution(mesh):
    split = P("tm", "rows", None, None)
    return jax.shard_map(
        functools.partial(local, mesh.shape["tm"], mesh.shape["rows"]),
        mesh=mesh,
        in_specs=(split, P(), split),
        out_specs=(split, split, P("rows", "tm")),
        check_vma=False,
    )
```

```python
import functools

import jax
import jax.numpy as jnp
from jax import lax
from jax.experimental import pallas as pl
from jax.experimental.pallas import tpu as pltpu
from jax.sharding import PartitionSpec as P

MESH = pl.DeviceIdType.MESH
F32 = jnp.float32
BF16 = jnp.bfloat16
VMEM_BYTES = (53 * 1024 + 576) * 1024


def along_width(lines, width):
    count, _, chans = lines.shape
    flat = lines.reshape(count * width, chans).astype(F32)
    column = lax.broadcasted_iota(jnp.int32, (count, width, chans), 1).reshape(flat.shape)
    before = jnp.where(column == 0, 0.0, pltpu.roll(flat, 1, 0)).astype(BF16)
    after = jnp.where(column == width - 1, 0.0, pltpu.roll(flat, count * width - 1, 0)).astype(BF16)
    return (
        before.reshape(lines.shape),
        lines,
        after.reshape(lines.shape),
    )


def kernel(
    nt, nr, reduce_here,
    video, weights, cot, act_out, igrad_out, kgrad_out,
    act, igrad, kgrad, taps, cot_own, seen, patches, gext, gpatches, total, chunks,
    s0, r0, a1, s1a, r1a, s1b, r1b, a2a, a2b, s2a, r2a, s2b, r2b, a3, s3, r3,
    local_sem, vsend, vrecv, gsend, grecv, ksend, krecv,
):
    frames, height, width, chans = video.shape
    rows = frames * height * width
    tm = lax.axis_index("tm")
    row = lax.axis_index("rows")

    def inside(dt, dr):
        return (tm + dt >= 0) & (tm + dt < nt) & (row + dr >= 0) & (row + dr < nr)

    def wrapped(dt, dr):
        return (lax.rem(tm + dt + nt, nt), lax.rem(row + dr + nr, nr))

    own, top, bottom = pl.ds(1, height), 0, height + 1
    old, new = pl.ds(0, 2), pl.ds(2, frames)
    loads = [
        pltpu.make_async_copy(video, seen.at[new, own], local_sem.at[0]),
        pltpu.make_async_copy(weights, taps, local_sem.at[1]),
        pltpu.make_async_copy(cot, cot_own, local_sem.at[2]),
    ]
    for load in loads:
        load.start()

    barrier = pltpu.get_barrier_semaphore()
    odd = lax.rem(tm, 2) == 1
    around = [(dt, dr) for dt in (-1, 0, 1) for dr in (-1, 0, 1) if dt or dr]
    expected = 0
    for dt, dr in around:
        greets = copies_to = inside(dt, dr)
        if dt and dr:
            greets = greets & (dt == -1) & jnp.logical_not(odd)
            copies_to = copies_to & (dt == 1) & odd
        expected = expected + jnp.where(copies_to, 1, 0)

        @pl.when(greets)
        def _(dt=dt, dr=dr):
            pl.semaphore_signal(barrier, inc=1, device_id=wrapped(dt, dr), device_id_type=MESH)

    if reduce_here:
        depth = lax.div(row, 2)
        side = lax.rem(row, 2)
        across = lax.div(tm, 2)
        core = lax.rem(tm, 2)
        other_core = (across * 2 + 1 - core, row)
        other_across = ((1 - across) * 2 + core, row)
        other_side = (tm, depth * 2 + 1 - side)
        layers = [lax.rem(depth + k, 4) for k in range(4)]
        partners = [other_across] + [(tm, layers[k] * 2 + side) for k in (1, 2, 3)]
        for partner in partners:
            pl.semaphore_signal(barrier, inc=1, device_id=partner, device_id_type=MESH)
        expected = expected + len(partners)
    pl.semaphore_wait(barrier, expected)

    def piece(dt, dr, send_when, source, target, sems, k):
        copy = pltpu.make_async_remote_copy(
            src_ref=source, dst_ref=target,
            send_sem=sems[0].at[k], recv_sem=sems[1].at[k],
            device_id=wrapped(dt, dr), device_id_type=MESH,
        )
        return (copy, send_when)

    def start(part):
        pl.when(part[1])(part[0].start)

    def sent(part):
        pl.when(part[1])(part[0].wait_send)

    def arrive(part, dt, dr, target):
        there = inside(dt, dr)
        pl.when(there)(part[0].wait_recv)

        @pl.when(jnp.logical_not(there))
        def _():
            target[...] = jnp.zeros(target.shape, BF16)

    last = pl.ds(frames - 2, 2)
    vsems, gsems = (vsend, vrecv), (gsend, grecv)
    halo = [
        piece(1, 0, inside(1, 0), video.at[last], seen.at[old, own], vsems, 0),
        piece(0, 1, inside(0, 1), video.at[:, height - 1], seen.at[new, top], vsems, 1),
        piece(0, -1, inside(0, -1), video.at[:, 0], seen.at[new, bottom], vsems, 2),
        piece(1, 1, inside(1, 1) & odd, video.at[last, height - 1], seen.at[old, top], vsems, 3),
        piece(1, -1, inside(1, -1) & odd, video.at[last, 0], seen.at[old, bottom], vsems, 4),
    ]
    for part in halo:
        start(part)
    even = jnp.logical_not(odd)
    newest = pl.ds(frames, 2)
    passed = [
        piece(1, 0, inside(1, -1) & even, seen.at[newest, top], seen.at[old, top], vsems, 3),
        piece(1, 0, inside(1, 1) & even, seen.at[newest, bottom], seen.at[old, bottom], vsems, 4),
    ]

    def spread(target, fr, ro, lines):
        flat = lines.reshape((-1,) + lines.shape[-2:])
        for c, piece in enumerate(along_width(flat, width)):
            target[fr, ro, :, c * chans:(c + 1) * chans] = piece.reshape(lines.shape)

    def patch(source, a, b):
        return source[a:a + frames, b:b + height].reshape(rows, 3 * chans)

    def forward(a, b):
        return jnp.dot(patch(patches, a, b), taps[a * 3 + b], preferred_element_type=F32)

    loads[0].wait()
    spread(patches, new, own, seen[new, own])
    loads[1].wait()
    pre = forward(2, 1)
    arrive(halo[0], -1, 0, seen.at[old, own])
    spread(patches, old, own, seen[old, own])
    pre = pre + forward(0, 1)
    pre = pre + forward(1, 1)
    arrive(halo[1], 0, -1, seen.at[new, top])
    start(passed[0])
    arrive(halo[2], 0, 1, seen.at[new, bottom])
    start(passed[1])
    spread(patches, new, top, seen[new, top])
    spread(patches, new, bottom, seen[new, bottom])
    pre = pre + forward(2, 0)
    pre = pre + forward(2, 2)
    arrive(halo[3], -1, -1, seen.at[old, top])
    spread(patches, old, top, seen[old, top])
    arrive(halo[4], -1, 1, seen.at[old, bottom])
    spread(patches, old, bottom, seen[old, bottom])
    for b in (0, 2):
        for a in range(2):
            pre = pre + forward(a, b)

    sig = 1.0 / (1.0 + jnp.exp(-pre))
    act[...] = (pre * sig).astype(BF16).reshape(act.shape)
    loads[2].wait()
    stores = [
        pltpu.make_async_copy(act, act_out, local_sem.at[3]),
        pltpu.make_async_copy(igrad, igrad_out, local_sem.at[4]),
        pltpu.make_async_copy(kgrad, kgrad_out, local_sem.at[5]),
    ]
    stores[0].start()
    cot_flat = cot_own[...].reshape(rows, chans).astype(F32)
    grad = (cot_flat * sig * (1.0 + pre * (1.0 - sig))).astype(BF16)
    mine, later = pl.ds(0, frames), pl.ds(frames, 2)
    early = pl.ds(0, 2)
    gext[mine, own] = grad.reshape(video.shape)
    ghalo = [
        piece(-1, 0, inside(-1, 0), gext.at[early, own], gext.at[later, own], gsems, 0),
        piece(0, 1, inside(0, 1), gext.at[mine, height], gext.at[mine, top], gsems, 1),
        piece(0, -1, inside(0, -1), gext.at[mine, 1], gext.at[mine, bottom], gsems, 2),
        piece(-1, 0, inside(-1, -1), gext.at[early, top], gext.at[later, top], gsems, 3),
        piece(-1, 0, inside(-1, 1), gext.at[early, bottom], gext.at[later, bottom], gsems, 4),
    ]
    for part in ghalo[:3]:
        start(part)

    turned = grad.astype(F32).T.astype(BF16)
    kdepth = 3 * chans

    def weight_part(k):
        total[:, k * kdepth:(k + 1) * kdepth] = jnp.dot(
            turned, patch(patches, k // 3, k % 3), preferred_element_type=F32
        )

    def backward(a, b):
        block = taps.at[(2 - a) * 3 + 2 - b]
        mat = jnp.concatenate(
            [block[(2 - c) * chans:(3 - c) * chans, :] for c in range(3)], axis=1
        )
        return lax.dot_general(
            patch(gpatches, a, b), mat, (((1,), (1,)), ((), ())), preferred_element_type=F32
        )

    def grad_own():
        spread(gpatches, mine, own, grad.reshape(video.shape))
        return backward(0, 1)

    def grad_later(out):
        arrive(ghalo[0], 1, 0, gext.at[later, own])
        spread(gpatches, later, own, gext[later, own])
        return out + backward(1, 1) + backward(2, 1)

    def grad_rows():
        arrive(ghalo[1], 0, -1, gext.at[mine, top])
        start(ghalo[3])
        arrive(ghalo[2], 0, 1, gext.at[mine, bottom])
        start(ghalo[4])

    def grad_edges(out):
        for ro in (top, bottom):
            spread(gpatches, mine, ro, gext[mine, ro])
        return out + backward(0, 0) + backward(0, 2)

    def grad_corners(out):
        arrive(ghalo[3], 1, -1, gext.at[later, top])
        spread(gpatches, later, top, gext[later, top])
        out = out + backward(1, 0) + backward(2, 0)
        arrive(ghalo[4], 1, 1, gext.at[later, bottom])
        spread(gpatches, later, bottom, gext[later, bottom])
        out = out + backward(1, 2) + backward(2, 2)
        igrad[...] = out.astype(BF16).reshape(igrad.shape)
        stores[1].start()

    def finish():
        for part in halo + passed + ghalo:
            sent(part)
        for store in stores:
            store.wait()

    if not reduce_here:
        for k in range(9):
            weight_part(k)
        kgrad[...] = total[...]
        stores[2].start()
        out = grad_later(grad_own())
        grad_rows()
        grad_corners(grad_edges(out))
        finish()
        return

    columns = total.shape[1] // nt
    wide = chunks.shape[-1]

    def cut(j):
        start = columns * j // 128 * 128
        shift = columns * j - start
        span = -(-(shift + columns) // 128) * 128
        piece = total[:, start:start + span]
        if shift:
            piece = pltpu.roll(piece, span - shift, 1)
        chunks[j] = piece[:, :wide].reshape(chunks.shape[1:])

    def send(k, source, target, device):
        copy = pltpu.make_async_remote_copy(
            src_ref=source, dst_ref=target,
            send_sem=ksend.at[k], recv_sem=krecv.at[k],
            device_id=device, device_id_type=MESH,
        )
        copy.start()
        return copy

    copies = []
    done = 0
    for half in range(2):
        need = -(-columns * (2 * half + 2) // kdepth)
        for k in range(done, need):
            weight_part(k)
        done = need
        cut(2 * half)
        cut(2 * half + 1)
        s0[half] = chunks[2 * half + 1 - core].astype(BF16)
        copies.append(send(half, s0.at[half], r0.at[half], other_core))

    out = grad_own()

    for half in range(2):
        copies[half].wait_recv()
        a1[half] = chunks[2 * half + core] + r0[half].astype(F32)
    s1a[...] = a1[1 - across, 0:2].astype(BF16)
    copies.append(send(2, s1a, r1a, other_across))
    s1b[...] = a1[:, 2:4, 1 - side].astype(BF16)
    copies.append(send(3, s1b, r1b, other_side))

    out = grad_later(out)

    copies[2].wait_recv()
    a2a[...] = a1[across, 0:2] + r1a[...].astype(F32)
    s2a[...] = a2a[:, 1 - side].astype(BF16)
    copies.append(send(4, s2a, r2a, other_side))
    copies[3].wait_recv()
    a2b[...] = a1[:, 2:4, side] + r1b[...].astype(F32)
    s2b[...] = a2b[1 - across].astype(BF16)
    copies.append(send(5, s2b, r2b, other_across))

    grad_rows()
    out = grad_edges(out)

    copies[4].wait_recv()
    a3[0:2] = a2a[:, side] + r2a[...].astype(F32)
    copies[5].wait_recv()
    a3[2:4] = a2b[across] + r2b[...].astype(F32)
    for k in (1, 2, 3):
        s3[k - 1] = a3[layers[k]].astype(BF16)
        copies.append(
            send(5 + k, s3.at[k - 1], r3.at[k - 1], (tm, layers[k] * 2 + side))
        )

    grad_corners(out)

    owned = a3[depth]
    for k in (1, 2, 3):
        copies[5 + k].wait_recv()
        owned = owned + r3[k - 1].astype(F32)
    kgrad[...] = owned[:, :columns]
    stores[2].start()
    for copy in copies:
        copy.wait_send()
    finish()


def deliver(*refs):
    count = (len(refs) - 1) // 2
    copies = [pltpu.make_async_copy(refs[k], refs[count + k], refs[-1].at[k]) for k in range(count)]
    for copy in copies:
        copy.start()
    for copy in copies:
        copy.wait()


def local(nt, nr, video, weights, cotangent):
    frames, height, width, chans = video.shape
    rows = frames * height * width
    cols = 27 * chans
    share, columns = chans // nr, cols // nt
    reduce_here = nt == 4 and nr == 8 and share % 16 == 0
    wide = -(-columns // 128) * 128 if reduce_here else 128
    sh = share if reduce_here else 16
    vm = pltpu.VMEM
    far = pl.BlockSpec(memory_space=pl.ANY)
    kshape = (share, columns) if reduce_here else (chans, cols)
    scratch = [
        vm(video.shape, BF16),
        vm(video.shape, BF16),
        vm(kshape, F32),
        vm((9, 3 * chans, chans), BF16),
        vm(video.shape, BF16),
        vm((frames + 2, height + 2, width, chans), BF16),
        vm((frames + 2, height + 2, width, 3 * chans), BF16),
        vm((frames + 2, height + 2, width, chans), BF16),
        vm((frames + 2, height + 2, width, 3 * chans), BF16),
        vm((chans, cols), F32),
        vm((4, 4, 2, sh, wide), F32),
        vm((2, 4, 2, sh, wide), BF16),
        vm((2, 4, 2, sh, wide), BF16),
        vm((2, 4, 2, sh, wide), F32),
        vm((2, 2, sh, wide), BF16),
        vm((2, 2, sh, wide), BF16),
        vm((2, 2, sh, wide), BF16),
        vm((2, 2, sh, wide), BF16),
        vm((2, 2, sh, wide), F32),
        vm((2, 2, sh, wide), F32),
        vm((2, sh, wide), BF16),
        vm((2, sh, wide), BF16),
        vm((2, sh, wide), BF16),
        vm((2, sh, wide), BF16),
        vm((4, sh, wide), F32),
        vm((3, sh, wide), BF16),
        vm((3, sh, wide), BF16),
        pltpu.SemaphoreType.DMA((6,)),
        pltpu.SemaphoreType.DMA((5,)),
        pltpu.SemaphoreType.DMA((5,)),
        pltpu.SemaphoreType.DMA((5,)),
        pltpu.SemaphoreType.DMA((5,)),
        pltpu.SemaphoreType.DMA((9,)),
        pltpu.SemaphoreType.DMA((9,)),
    ]
    activated, input_grad, kgrad = pl.pallas_call(
        functools.partial(kernel, nt, nr, reduce_here),
        out_shape=(
            jax.ShapeDtypeStruct(video.shape, BF16),
            jax.ShapeDtypeStruct(video.shape, BF16),
            jax.ShapeDtypeStruct(kshape, F32),
        ),
        in_specs=[far, far, far],
        out_specs=(far, far, far),
        scratch_shapes=scratch,
        compiler_params=pltpu.CompilerParams(
            collective_id=0, has_side_effects=True, vmem_limit_bytes=VMEM_BYTES
        ),
        cost_estimate=pl.CostEstimate(
            flops=6 * rows * cols * chans, bytes_accessed=4 * 1024 * 1024, transcendentals=rows * chans
        ),
        name="conv_silu_grads",
    )(video, weights.reshape(9, 3 * chans, chans), cotangent)
    if not reduce_here:
        kgrad = lax.psum_scatter(kgrad, "rows", scatter_dimension=0, tiled=True)
        kgrad = lax.psum_scatter(kgrad, "tm", scatter_dimension=1, tiled=True)
        return activated, input_grad, kgrad
    results = (activated, input_grad, kgrad)
    return pl.pallas_call(
        deliver,
        out_shape=tuple(jax.ShapeDtypeStruct(x.shape, x.dtype) for x in results),
        in_specs=[pl.BlockSpec(memory_space=pltpu.VMEM)] * 3,
        out_specs=(far,) * 3,
        scratch_shapes=[pltpu.SemaphoreType.DMA((3,))],
        compiler_params=pltpu.CompilerParams(vmem_limit_bytes=4 * 1024 * 1024),
        name="deliver",
    )(*results)


def solution(mesh):
    split = P("tm", "rows", None, None)
    return jax.shard_map(
        functools.partial(local, mesh.shape["tm"], mesh.shape["rows"]),
        mesh=mesh,
        in_specs=(split, P(), split),
        out_specs=(split, split, P("rows", "tm")),
        check_vma=False,
    )
```

```python
import functools

import jax
import jax.numpy as jnp
from jax import lax
from jax.experimental import pallas as pl
from jax.experimental.pallas import tpu as pltpu
from jax.sharding import PartitionSpec as P

MESH = pl.DeviceIdType.MESH
F32 = jnp.float32
BF16 = jnp.bfloat16
VMEM_BYTES = (53 * 1024 + 576) * 1024


def along_width(lines, width):
    count, _, chans = lines.shape
    flat = lines.reshape(count * width, chans).astype(F32)
    column = lax.broadcasted_iota(jnp.int32, (count, width, chans), 1).reshape(flat.shape)
    before = jnp.where(column == 0, 0.0, pltpu.roll(flat, 1, 0)).astype(BF16)
    after = jnp.where(column == width - 1, 0.0, pltpu.roll(flat, count * width - 1, 0)).astype(BF16)
    return (
        before.reshape(lines.shape),
        lines,
        after.reshape(lines.shape),
    )


def kernel(
    nt, nr, reduce_here,
    video, weights, cot, act, igrad, kgrad,
    taps, cot_own, seen, patches, gext, gpatches, total, chunks,
    s0, r0, a1, s1a, r1a, s1b, r1b, a2a, a2b, s2a, r2a, s2b, r2b, a3, s3, r3,
    local_sem, vsend, vrecv, gsend, grecv, ksend, krecv,
):
    frames, height, width, chans = video.shape
    rows = frames * height * width
    tm = lax.axis_index("tm")
    row = lax.axis_index("rows")

    def inside(dt, dr):
        return (tm + dt >= 0) & (tm + dt < nt) & (row + dr >= 0) & (row + dr < nr)

    def wrapped(dt, dr):
        return (lax.rem(tm + dt + nt, nt), lax.rem(row + dr + nr, nr))

    own, top, bottom = pl.ds(1, height), 0, height + 1
    old, new = pl.ds(0, 2), pl.ds(2, frames)
    loads = [
        pltpu.make_async_copy(video, seen.at[new, own], local_sem.at[0]),
        pltpu.make_async_copy(weights, taps, local_sem.at[1]),
        pltpu.make_async_copy(cot, cot_own, local_sem.at[2]),
    ]
    for load in loads:
        load.start()

    barrier = pltpu.get_barrier_semaphore()
    odd = lax.rem(tm, 2) == 1
    around = [(dt, dr) for dt in (-1, 0, 1) for dr in (-1, 0, 1) if dt or dr]
    expected = 0
    for dt, dr in around:
        greets = copies_to = inside(dt, dr)
        if dt and dr:
            greets = greets & (dt == -1) & jnp.logical_not(odd)
            copies_to = copies_to & (dt == 1) & odd
        expected = expected + jnp.where(copies_to, 1, 0)

        @pl.when(greets)
        def _(dt=dt, dr=dr):
            pl.semaphore_signal(barrier, inc=1, device_id=wrapped(dt, dr), device_id_type=MESH)

    if reduce_here:
        depth = lax.div(row, 2)
        side = lax.rem(row, 2)
        across = lax.div(tm, 2)
        core = lax.rem(tm, 2)
        other_core = (across * 2 + 1 - core, row)
        other_across = ((1 - across) * 2 + core, row)
        other_side = (tm, depth * 2 + 1 - side)
        layers = [lax.rem(depth + k, 4) for k in range(4)]
        partners = [other_across] + [(tm, layers[k] * 2 + side) for k in (1, 2, 3)]
        for partner in partners:
            pl.semaphore_signal(barrier, inc=1, device_id=partner, device_id_type=MESH)
        expected = expected + len(partners)
    pl.semaphore_wait(barrier, expected)

    def piece(dt, dr, send_when, source, target, sems, k):
        copy = pltpu.make_async_remote_copy(
            src_ref=source, dst_ref=target,
            send_sem=sems[0].at[k], recv_sem=sems[1].at[k],
            device_id=wrapped(dt, dr), device_id_type=MESH,
        )
        return (copy, send_when)

    def start(part):
        pl.when(part[1])(part[0].start)

    def sent(part):
        pl.when(part[1])(part[0].wait_send)

    def arrive(part, dt, dr, target):
        there = inside(dt, dr)
        pl.when(there)(part[0].wait_recv)

        @pl.when(jnp.logical_not(there))
        def _():
            target[...] = jnp.zeros(target.shape, BF16)

    last = pl.ds(frames - 2, 2)
    vsems, gsems = (vsend, vrecv), (gsend, grecv)
    halo = [
        piece(1, 0, inside(1, 0), video.at[last], seen.at[old, own], vsems, 0),
        piece(0, 1, inside(0, 1), video.at[:, height - 1], seen.at[new, top], vsems, 1),
        piece(0, -1, inside(0, -1), video.at[:, 0], seen.at[new, bottom], vsems, 2),
        piece(1, 1, inside(1, 1) & odd, video.at[last, height - 1], seen.at[old, top], vsems, 3),
        piece(1, -1, inside(1, -1) & odd, video.at[last, 0], seen.at[old, bottom], vsems, 4),
    ]
    for part in halo:
        start(part)
    even = jnp.logical_not(odd)
    newest = pl.ds(frames, 2)
    passed = [
        piece(1, 0, inside(1, -1) & even, seen.at[newest, top], seen.at[old, top], vsems, 3),
        piece(1, 0, inside(1, 1) & even, seen.at[newest, bottom], seen.at[old, bottom], vsems, 4),
    ]

    def spread(target, fr, ro, lines):
        flat = lines.reshape((-1,) + lines.shape[-2:])
        for c, piece in enumerate(along_width(flat, width)):
            target[fr, ro, :, c * chans:(c + 1) * chans] = piece.reshape(lines.shape)

    def patch(source, a, b):
        return source[a:a + frames, b:b + height].reshape(rows, 3 * chans)

    def forward(a, b):
        return jnp.dot(patch(patches, a, b), taps[a * 3 + b], preferred_element_type=F32)

    loads[0].wait()
    spread(patches, new, own, seen[new, own])
    loads[1].wait()
    pre = forward(2, 1)
    arrive(halo[0], -1, 0, seen.at[old, own])
    spread(patches, old, own, seen[old, own])
    pre = pre + forward(0, 1)
    pre = pre + forward(1, 1)
    arrive(halo[1], 0, -1, seen.at[new, top])
    start(passed[0])
    arrive(halo[2], 0, 1, seen.at[new, bottom])
    start(passed[1])
    spread(patches, new, top, seen[new, top])
    spread(patches, new, bottom, seen[new, bottom])
    pre = pre + forward(2, 0)
    pre = pre + forward(2, 2)
    arrive(halo[3], -1, -1, seen.at[old, top])
    spread(patches, old, top, seen[old, top])
    arrive(halo[4], -1, 1, seen.at[old, bottom])
    spread(patches, old, bottom, seen[old, bottom])
    for b in (0, 2):
        for a in range(2):
            pre = pre + forward(a, b)

    sig = 1.0 / (1.0 + jnp.exp(-pre))
    act[...] = (pre * sig).astype(BF16).reshape(act.shape)
    loads[2].wait()
    cot_flat = cot_own[...].reshape(rows, chans).astype(F32)
    grad = (cot_flat * sig * (1.0 + pre * (1.0 - sig))).astype(BF16)
    mine, later = pl.ds(0, frames), pl.ds(frames, 2)
    early = pl.ds(0, 2)
    gext[mine, own] = grad.reshape(video.shape)
    ghalo = [
        piece(-1, 0, inside(-1, 0), gext.at[early, own], gext.at[later, own], gsems, 0),
        piece(0, 1, inside(0, 1), gext.at[mine, height], gext.at[mine, top], gsems, 1),
        piece(0, -1, inside(0, -1), gext.at[mine, 1], gext.at[mine, bottom], gsems, 2),
        piece(-1, 0, inside(-1, -1), gext.at[early, top], gext.at[later, top], gsems, 3),
        piece(-1, 0, inside(-1, 1), gext.at[early, bottom], gext.at[later, bottom], gsems, 4),
    ]
    for part in ghalo[:3]:
        start(part)

    turned = grad.astype(F32).T.astype(BF16)
    kdepth = 3 * chans

    def weight_part(k):
        total[:, k * kdepth:(k + 1) * kdepth] = jnp.dot(
            turned, patch(patches, k // 3, k % 3), preferred_element_type=F32
        )

    def backward(a, b):
        block = taps.at[(2 - a) * 3 + 2 - b]
        mat = jnp.concatenate(
            [block[(2 - c) * chans:(3 - c) * chans, :] for c in range(3)], axis=1
        )
        return lax.dot_general(
            patch(gpatches, a, b), mat, (((1,), (1,)), ((), ())), preferred_element_type=F32
        )

    def grad_own():
        spread(gpatches, mine, own, grad.reshape(video.shape))
        return backward(0, 1)

    def grad_later(out):
        arrive(ghalo[0], 1, 0, gext.at[later, own])
        spread(gpatches, later, own, gext[later, own])
        return out + backward(1, 1) + backward(2, 1)

    def grad_rows():
        arrive(ghalo[1], 0, -1, gext.at[mine, top])
        start(ghalo[3])
        arrive(ghalo[2], 0, 1, gext.at[mine, bottom])
        start(ghalo[4])

    def grad_edges(out):
        for ro in (top, bottom):
            spread(gpatches, mine, ro, gext[mine, ro])
        return out + backward(0, 0) + backward(0, 2)

    def grad_corners(out):
        arrive(ghalo[3], 1, -1, gext.at[later, top])
        spread(gpatches, later, top, gext[later, top])
        out = out + backward(1, 0) + backward(2, 0)
        arrive(ghalo[4], 1, 1, gext.at[later, bottom])
        spread(gpatches, later, bottom, gext[later, bottom])
        out = out + backward(1, 2) + backward(2, 2)
        igrad[...] = out.astype(BF16).reshape(igrad.shape)

    def finish():
        for part in halo + passed + ghalo:
            sent(part)

    if not reduce_here:
        for k in range(9):
            weight_part(k)
        kgrad[...] = total[...]
        out = grad_later(grad_own())
        grad_rows()
        grad_corners(grad_edges(out))
        finish()
        return

    columns = total.shape[1] // nt
    wide = chunks.shape[-1]

    def cut(j):
        start = columns * j // 128 * 128
        shift = columns * j - start
        span = -(-(shift + columns) // 128) * 128
        piece = total[:, start:start + span]
        if shift:
            piece = pltpu.roll(piece, span - shift, 1)
        chunks[j] = piece[:, :wide].reshape(chunks.shape[1:])

    def send(k, source, target, device):
        copy = pltpu.make_async_remote_copy(
            src_ref=source, dst_ref=target,
            send_sem=ksend.at[k], recv_sem=krecv.at[k],
            device_id=device, device_id_type=MESH,
        )
        copy.start()
        return copy

    copies = []
    done = 0
    for half in range(2):
        need = -(-columns * (2 * half + 2) // kdepth)
        for k in range(done, need):
            weight_part(k)
        done = need
        cut(2 * half)
        cut(2 * half + 1)
        s0[half] = chunks[2 * half + 1 - core].astype(BF16)
        copies.append(send(half, s0.at[half], r0.at[half], other_core))

    out = grad_own()

    for half in range(2):
        copies[half].wait_recv()
        a1[half] = chunks[2 * half + core] + r0[half].astype(F32)
    s1a[...] = a1[1 - across, 0:2].astype(BF16)
    copies.append(send(2, s1a, r1a, other_across))
    s1b[...] = a1[:, 2:4, 1 - side].astype(BF16)
    copies.append(send(3, s1b, r1b, other_side))

    grad_rows()
    out = grad_later(out)

    copies[2].wait_recv()
    a2a[...] = a1[across, 0:2] + r1a[...].astype(F32)
    s2a[...] = a2a[:, 1 - side].astype(BF16)
    copies.append(send(4, s2a, r2a, other_side))
    copies[3].wait_recv()
    a2b[...] = a1[:, 2:4, side] + r1b[...].astype(F32)
    s2b[...] = a2b[1 - across].astype(BF16)
    copies.append(send(5, s2b, r2b, other_across))

    out = grad_edges(out)

    copies[4].wait_recv()
    a3[0:2] = a2a[:, side] + r2a[...].astype(F32)
    copies[5].wait_recv()
    a3[2:4] = a2b[across] + r2b[...].astype(F32)
    for k in (1, 2, 3):
        s3[k - 1] = a3[layers[k]].astype(BF16)
        copies.append(
            send(5 + k, s3.at[k - 1], r3.at[k - 1], (tm, layers[k] * 2 + side))
        )

    grad_corners(out)

    owned = a3[depth]
    for k in (1, 2, 3):
        copies[5 + k].wait_recv()
        owned = owned + r3[k - 1].astype(F32)
    kgrad[...] = owned[:, :columns]
    for copy in copies:
        copy.wait_send()
    finish()


def deliver(*refs):
    count = (len(refs) - 1) // 2
    copies = [pltpu.make_async_copy(refs[k], refs[count + k], refs[-1].at[k]) for k in range(count)]
    for copy in copies:
        copy.start()
    for copy in copies:
        copy.wait()


def local(nt, nr, video, weights, cotangent):
    frames, height, width, chans = video.shape
    rows = frames * height * width
    cols = 27 * chans
    share, columns = chans // nr, cols // nt
    reduce_here = nt == 4 and nr == 8 and share % 16 == 0
    wide = -(-columns // 128) * 128 if reduce_here else 128
    sh = share if reduce_here else 16
    vm = pltpu.VMEM
    far = pl.BlockSpec(memory_space=pl.ANY)
    kshape = (share, columns) if reduce_here else (chans, cols)
    scratch = [
        vm((9, 3 * chans, chans), BF16),
        vm(video.shape, BF16),
        vm((frames + 2, height + 2, width, chans), BF16),
        vm((frames + 2, height + 2, width, 3 * chans), BF16),
        vm((frames + 2, height + 2, width, chans), BF16),
        vm((frames + 2, height + 2, width, 3 * chans), BF16),
        vm((chans, cols), F32),
        vm((4, 4, 2, sh, wide), F32),
        vm((2, 4, 2, sh, wide), BF16),
        vm((2, 4, 2, sh, wide), BF16),
        vm((2, 4, 2, sh, wide), F32),
        vm((2, 2, sh, wide), BF16),
        vm((2, 2, sh, wide), BF16),
        vm((2, 2, sh, wide), BF16),
        vm((2, 2, sh, wide), BF16),
        vm((2, 2, sh, wide), F32),
        vm((2, 2, sh, wide), F32),
        vm((2, sh, wide), BF16),
        vm((2, sh, wide), BF16),
        vm((2, sh, wide), BF16),
        vm((2, sh, wide), BF16),
        vm((4, sh, wide), F32),
        vm((3, sh, wide), BF16),
        vm((3, sh, wide), BF16),
        pltpu.SemaphoreType.DMA((3,)),
        pltpu.SemaphoreType.DMA((5,)),
        pltpu.SemaphoreType.DMA((5,)),
        pltpu.SemaphoreType.DMA((5,)),
        pltpu.SemaphoreType.DMA((5,)),
        pltpu.SemaphoreType.DMA((9,)),
        pltpu.SemaphoreType.DMA((9,)),
    ]
    activated, input_grad, kgrad = pl.pallas_call(
        functools.partial(kernel, nt, nr, reduce_here),
        out_shape=(
            jax.ShapeDtypeStruct(video.shape, BF16),
            jax.ShapeDtypeStruct(video.shape, BF16),
            jax.ShapeDtypeStruct(kshape, F32),
        ),
        in_specs=[far, far, far],
        out_specs=(pl.BlockSpec(memory_space=pltpu.VMEM),) * 3,
        scratch_shapes=scratch,
        compiler_params=pltpu.CompilerParams(
            collective_id=0, has_side_effects=True, vmem_limit_bytes=VMEM_BYTES
        ),
        cost_estimate=pl.CostEstimate(
            flops=6 * rows * cols * chans, bytes_accessed=4 * 1024 * 1024, transcendentals=rows * chans
        ),
        name="conv_silu_grads",
    )(video, weights.reshape(9, 3 * chans, chans), cotangent)
    if not reduce_here:
        kgrad = lax.psum_scatter(kgrad, "rows", scatter_dimension=0, tiled=True)
        kgrad = lax.psum_scatter(kgrad, "tm", scatter_dimension=1, tiled=True)
        return activated, input_grad, kgrad
    results = (activated, input_grad, kgrad)
    return pl.pallas_call(
        deliver,
        out_shape=tuple(jax.ShapeDtypeStruct(x.shape, x.dtype) for x in results),
        in_specs=[pl.BlockSpec(memory_space=pltpu.VMEM)] * 3,
        out_specs=(far,) * 3,
        scratch_shapes=[pltpu.SemaphoreType.DMA((3,))],
        compiler_params=pltpu.CompilerParams(vmem_limit_bytes=4 * 1024 * 1024),
        name="deliver",
    )(*results)


def solution(mesh):
    split = P("tm", "rows", None, None)
    return jax.shard_map(
        functools.partial(local, mesh.shape["tm"], mesh.shape["rows"]),
        mesh=mesh,
        in_specs=(split, P(), split),
        out_specs=(split, split, P("rows", "tm")),
        check_vma=False,
    )
```

```python
import functools

import jax
import jax.numpy as jnp
from jax import lax
from jax.experimental import pallas as pl
from jax.experimental.pallas import tpu as pltpu
from jax.sharding import PartitionSpec as P

MESH = pl.DeviceIdType.MESH
F32 = jnp.float32
BF16 = jnp.bfloat16
VMEM_BYTES = (53 * 1024 + 576) * 1024


def along_width(lines, width):
    count, _, chans = lines.shape
    flat = lines.reshape(count * width, chans).astype(F32)
    column = lax.broadcasted_iota(jnp.int32, (count, width, chans), 1).reshape(flat.shape)
    before = jnp.where(column == 0, 0.0, pltpu.roll(flat, 1, 0)).astype(BF16)
    after = jnp.where(column == width - 1, 0.0, pltpu.roll(flat, count * width - 1, 0)).astype(BF16)
    return (
        before.reshape(lines.shape),
        lines,
        after.reshape(lines.shape),
    )


def kernel(
    nt, nr, reduce_here,
    video, weights, cot, act, igrad, kgrad,
    taps, cot_own, seen, patches, gext, gpatches, total, chunks,
    s0, r0, s1a, r1a, s1b, r1b, s2a, r2a, s2b, r2b, a3, s3, r3,
    local_sem, vsend, vrecv, gsend, grecv, ksend, krecv,
):
    frames, height, width, chans = video.shape
    rows = frames * height * width
    tm = lax.axis_index("tm")
    row = lax.axis_index("rows")

    def inside(dt, dr):
        return (tm + dt >= 0) & (tm + dt < nt) & (row + dr >= 0) & (row + dr < nr)

    def wrapped(dt, dr):
        return (lax.rem(tm + dt + nt, nt), lax.rem(row + dr + nr, nr))

    own, top, bottom = pl.ds(1, height), 0, height + 1
    old, new = pl.ds(0, 2), pl.ds(2, frames)
    loads = [
        pltpu.make_async_copy(video, seen.at[new, own], local_sem.at[0]),
        pltpu.make_async_copy(weights, taps, local_sem.at[1]),
        pltpu.make_async_copy(cot, cot_own, local_sem.at[2]),
    ]
    for load in loads:
        load.start()

    barrier = pltpu.get_barrier_semaphore()
    odd = lax.rem(tm, 2) == 1
    around = [(dt, dr) for dt in (-1, 0, 1) for dr in (-1, 0, 1) if dt or dr]
    expected = 0
    for dt, dr in around:
        greets = copies_to = inside(dt, dr)
        if dt and dr:
            greets = greets & (dt == -1) & jnp.logical_not(odd)
            copies_to = copies_to & (dt == 1) & odd
        expected = expected + jnp.where(copies_to, 1, 0)

        @pl.when(greets)
        def _(dt=dt, dr=dr):
            pl.semaphore_signal(barrier, inc=1, device_id=wrapped(dt, dr), device_id_type=MESH)

    if reduce_here:
        depth = lax.div(row, 2)
        side = lax.rem(row, 2)
        across = lax.div(tm, 2)
        core = lax.rem(tm, 2)
        other_core = (across * 2 + 1 - core, row)
        other_across = ((1 - across) * 2 + core, row)
        other_side = (tm, depth * 2 + 1 - side)
        layers = [lax.rem(depth + k, 4) for k in range(4)]
        partners = [other_across] + [(tm, layers[k] * 2 + side) for k in (1, 2, 3)]
        for partner in partners:
            pl.semaphore_signal(barrier, inc=1, device_id=partner, device_id_type=MESH)
        expected = expected + len(partners)
    pl.semaphore_wait(barrier, expected)

    def piece(dt, dr, send_when, source, target, sems, k):
        copy = pltpu.make_async_remote_copy(
            src_ref=source, dst_ref=target,
            send_sem=sems[0].at[k], recv_sem=sems[1].at[k],
            device_id=wrapped(dt, dr), device_id_type=MESH,
        )
        return (copy, send_when)

    def start(part, also=True):
        pl.when(part[1] & also)(part[0].start)

    def sent(part):
        pl.when(part[1])(part[0].wait_send)

    def arrive(part, dt, dr, target):
        there = inside(dt, dr)
        pl.when(there)(part[0].wait_recv)

        @pl.when(jnp.logical_not(there))
        def _():
            target[...] = jnp.zeros(target.shape, BF16)

    last = pl.ds(frames - 2, 2)
    vsems, gsems = (vsend, vrecv), (gsend, grecv)
    halo = [
        piece(1, 0, inside(1, 0), video.at[last], seen.at[old, own], vsems, 0),
        piece(0, 1, inside(0, 1), video.at[:, height - 1], seen.at[new, top], vsems, 1),
        piece(0, -1, inside(0, -1), video.at[:, 0], seen.at[new, bottom], vsems, 2),
        piece(1, 1, inside(1, 1) & odd, video.at[last, height - 1], seen.at[old, top], vsems, 3),
        piece(1, -1, inside(1, -1) & odd, video.at[last, 0], seen.at[old, bottom], vsems, 4),
    ]
    even = jnp.logical_not(odd)
    start(halo[0])
    start(halo[1], even)
    start(halo[2], even)
    newest = pl.ds(frames, 2)
    passed = [
        piece(1, 0, inside(1, -1) & even, seen.at[newest, top], seen.at[old, top], vsems, 3),
        piece(1, 0, inside(1, 1) & even, seen.at[newest, bottom], seen.at[old, bottom], vsems, 4),
    ]

    def spread(target, fr, ro, lines):
        flat = lines.reshape((-1,) + lines.shape[-2:])
        for c, piece in enumerate(along_width(flat, width)):
            target[fr, ro, :, c * chans:(c + 1) * chans] = piece.reshape(lines.shape)

    def patch(source, a, b):
        return source[a:a + frames, b:b + height].reshape(rows, 3 * chans)

    def forward(a, b):
        return jnp.dot(patch(patches, a, b), taps[a * 3 + b], preferred_element_type=F32)

    loads[0].wait()
    spread(patches, new, own, seen[new, own])
    start(halo[1], odd)
    start(halo[2], odd)
    start(halo[3])
    start(halo[4])
    loads[1].wait()
    pre = forward(2, 1)
    arrive(halo[0], -1, 0, seen.at[old, own])
    spread(patches, old, own, seen[old, own])
    pre = pre + forward(0, 1)
    pre = pre + forward(1, 1)
    arrive(halo[1], 0, -1, seen.at[new, top])
    start(passed[0])
    arrive(halo[2], 0, 1, seen.at[new, bottom])
    start(passed[1])
    spread(patches, new, top, seen[new, top])
    spread(patches, new, bottom, seen[new, bottom])
    pre = pre + forward(2, 0)
    pre = pre + forward(2, 2)
    arrive(halo[3], -1, -1, seen.at[old, top])
    spread(patches, old, top, seen[old, top])
    arrive(halo[4], -1, 1, seen.at[old, bottom])
    spread(patches, old, bottom, seen[old, bottom])
    for b in (0, 2):
        for a in range(2):
            pre = pre + forward(a, b)

    sig = 1.0 / (1.0 + jnp.exp(-pre))
    act[...] = (pre * sig).astype(BF16).reshape(act.shape)
    loads[2].wait()
    cot_flat = cot_own[...].reshape(rows, chans).astype(F32)
    grad = (cot_flat * sig * (1.0 + pre * (1.0 - sig))).astype(BF16)
    mine, later = pl.ds(0, frames), pl.ds(frames, 2)
    early = pl.ds(0, 2)
    gext[mine, own] = grad.reshape(video.shape)
    ghalo = [
        piece(-1, 0, inside(-1, 0), gext.at[early, own], gext.at[later, own], gsems, 0),
        piece(0, 1, inside(0, 1), gext.at[mine, height], gext.at[mine, top], gsems, 1),
        piece(0, -1, inside(0, -1), gext.at[mine, 1], gext.at[mine, bottom], gsems, 2),
        piece(-1, 0, inside(-1, -1), gext.at[early, top], gext.at[later, top], gsems, 3),
        piece(-1, 0, inside(-1, 1), gext.at[early, bottom], gext.at[later, bottom], gsems, 4),
    ]
    for part in ghalo[:3]:
        start(part)

    turned = grad.astype(F32).T.astype(BF16)
    kdepth = 3 * chans

    def weight_part(k):
        total[:, k * kdepth:(k + 1) * kdepth] = jnp.dot(
            turned, patch(patches, k // 3, k % 3), preferred_element_type=F32
        )

    def backward(a, b):
        block = taps.at[(2 - a) * 3 + 2 - b]
        mat = jnp.concatenate(
            [block[(2 - c) * chans:(3 - c) * chans, :] for c in range(3)], axis=1
        )
        return lax.dot_general(
            patch(gpatches, a, b), mat, (((1,), (1,)), ((), ())), preferred_element_type=F32
        )

    def grad_own():
        spread(gpatches, mine, own, grad.reshape(video.shape))
        return backward(0, 1)

    def grad_later(out):
        arrive(ghalo[0], 1, 0, gext.at[later, own])
        spread(gpatches, later, own, gext[later, own])
        return out + backward(1, 1) + backward(2, 1)

    def grad_rows():
        arrive(ghalo[1], 0, -1, gext.at[mine, top])
        start(ghalo[3])
        arrive(ghalo[2], 0, 1, gext.at[mine, bottom])
        start(ghalo[4])

    def grad_edges(out):
        for ro in (top, bottom):
            spread(gpatches, mine, ro, gext[mine, ro])
        return out + backward(0, 0) + backward(0, 2)

    def grad_corners(out):
        arrive(ghalo[3], 1, -1, gext.at[later, top])
        spread(gpatches, later, top, gext[later, top])
        out = out + backward(1, 0) + backward(2, 0)
        arrive(ghalo[4], 1, 1, gext.at[later, bottom])
        spread(gpatches, later, bottom, gext[later, bottom])
        out = out + backward(1, 2) + backward(2, 2)
        igrad[...] = out.astype(BF16).reshape(igrad.shape)

    def finish():
        for part in halo + passed + ghalo:
            sent(part)

    if not reduce_here:
        for k in range(9):
            weight_part(k)
        kgrad[...] = total[...]
        out = grad_later(grad_own())
        grad_rows()
        grad_corners(grad_edges(out))
        finish()
        return

    columns = total.shape[1] // nt
    wide = chunks.shape[-1]

    def cut(j):
        start = columns * j // 128 * 128
        shift = columns * j - start
        span = -(-(shift + columns) // 128) * 128
        piece = total[:, start:start + span]
        if shift:
            piece = pltpu.roll(piece, span - shift, 1)
        chunks[j] = piece[:, :wide].reshape(chunks.shape[1:])

    def send(k, source, target, device):
        copy = pltpu.make_async_remote_copy(
            src_ref=source, dst_ref=target,
            send_sem=ksend.at[k], recv_sem=krecv.at[k],
            device_id=device, device_id_type=MESH,
        )
        copy.start()
        return copy

    halves = [
        pltpu.make_async_remote_copy(
            src_ref=s0.at[half], dst_ref=r0.at[half],
            send_sem=ksend.at[half], recv_sem=krecv.at[half],
            device_id=other_core, device_id_type=MESH,
        )
        for half in range(2)
    ]
    copies = list(halves)
    done = 0
    for j in range(nt):
        need = -(-columns * (j + 1) // kdepth)
        for k in range(done, need):
            weight_part(k)
        done = need
        cut(j)

        @pl.when(core != j % 2)
        def _(j=j):
            s0[j // 2] = chunks[j].astype(BF16)
            halves[j // 2].start()

    out = grad_own()

    near, away = across * 2 + core, (1 - across) * 2 + core
    for half in halves:
        half.wait_recv()
    s1a[...] = (chunks[away, 0:2] + r0[1 - across, 0:2].astype(F32)).astype(BF16)
    copies.append(send(2, s1a, r1a, other_across))
    for half in range(2):
        s1b[half] = (
            chunks[half * 2 + core, 2:4, 1 - side] + r0[half, 2:4, 1 - side].astype(F32)
        ).astype(BF16)
    copies.append(send(3, s1b, r1b, other_side))

    grad_rows()
    out = grad_later(out)

    copies[2].wait_recv()
    s2a[...] = (
        chunks[near, 0:2, 1 - side] + r0[across, 0:2, 1 - side].astype(F32)
        + r1a[:, 1 - side].astype(F32)
    ).astype(BF16)
    copies.append(send(4, s2a, r2a, other_side))
    copies[3].wait_recv()
    s2b[...] = (
        chunks[away, 2:4, side] + r0[1 - across, 2:4, side].astype(F32)
        + r1b[1 - across].astype(F32)
    ).astype(BF16)
    copies.append(send(5, s2b, r2b, other_across))
    a3[0:2] = (
        chunks[near, 0:2, side] + r0[across, 0:2, side].astype(F32) + r1a[:, side].astype(F32)
    )
    a3[2:4] = (
        chunks[near, 2:4, side] + r0[across, 2:4, side].astype(F32) + r1b[across].astype(F32)
    )

    out = grad_edges(out)

    copies[4].wait_recv()
    a3[0:2] = a3[0:2] + r2a[...].astype(F32)
    copies[5].wait_recv()
    a3[2:4] = a3[2:4] + r2b[...].astype(F32)
    for k in (1, 2, 3):
        s3[k - 1] = a3[layers[k]].astype(BF16)
        copies.append(
            send(5 + k, s3.at[k - 1], r3.at[k - 1], (tm, layers[k] * 2 + side))
        )

    grad_corners(out)

    owned = a3[depth]
    for k in (1, 2, 3):
        copies[5 + k].wait_recv()
        owned = owned + r3[k - 1].astype(F32)
    kgrad[...] = owned[:, :columns]
    for copy in copies:
        copy.wait_send()
    finish()


def deliver(*refs):
    count = (len(refs) - 1) // 2
    copies = [pltpu.make_async_copy(refs[k], refs[count + k], refs[-1].at[k]) for k in range(count)]
    for copy in copies:
        copy.start()
    for copy in copies:
        copy.wait()


def local(nt, nr, video, weights, cotangent):
    frames, height, width, chans = video.shape
    rows = frames * height * width
    cols = 27 * chans
    share, columns = chans // nr, cols // nt
    reduce_here = nt == 4 and nr == 8 and share % 16 == 0
    wide = -(-columns // 128) * 128 if reduce_here else 128
    sh = share if reduce_here else 16
    vm = pltpu.VMEM
    far = pl.BlockSpec(memory_space=pl.ANY)
    kshape = (share, columns) if reduce_here else (chans, cols)
    scratch = [
        vm((9, 3 * chans, chans), BF16),
        vm(video.shape, BF16),
        vm((frames + 2, height + 2, width, chans), BF16),
        vm((frames + 2, height + 2, width, 3 * chans), BF16),
        vm((frames + 2, height + 2, width, chans), BF16),
        vm((frames + 2, height + 2, width, 3 * chans), BF16),
        vm((chans, cols), F32),
        vm((4, 4, 2, sh, wide), F32),
        vm((2, 4, 2, sh, wide), BF16),
        vm((2, 4, 2, sh, wide), BF16),
        vm((2, 2, sh, wide), BF16),
        vm((2, 2, sh, wide), BF16),
        vm((2, 2, sh, wide), BF16),
        vm((2, 2, sh, wide), BF16),
        vm((2, sh, wide), BF16),
        vm((2, sh, wide), BF16),
        vm((2, sh, wide), BF16),
        vm((2, sh, wide), BF16),
        vm((4, sh, wide), F32),
        vm((3, sh, wide), BF16),
        vm((3, sh, wide), BF16),
        pltpu.SemaphoreType.DMA((3,)),
        pltpu.SemaphoreType.DMA((5,)),
        pltpu.SemaphoreType.DMA((5,)),
        pltpu.SemaphoreType.DMA((5,)),
        pltpu.SemaphoreType.DMA((5,)),
        pltpu.SemaphoreType.DMA((9,)),
        pltpu.SemaphoreType.DMA((9,)),
    ]
    activated, input_grad, kgrad = pl.pallas_call(
        functools.partial(kernel, nt, nr, reduce_here),
        out_shape=(
            jax.ShapeDtypeStruct(video.shape, BF16),
            jax.ShapeDtypeStruct(video.shape, BF16),
            jax.ShapeDtypeStruct(kshape, F32),
        ),
        in_specs=[far, far, far],
        out_specs=(pl.BlockSpec(memory_space=pltpu.VMEM),) * 3,
        scratch_shapes=scratch,
        compiler_params=pltpu.CompilerParams(
            collective_id=0, has_side_effects=True, vmem_limit_bytes=VMEM_BYTES
        ),
        cost_estimate=pl.CostEstimate(
            flops=6 * rows * cols * chans, bytes_accessed=4 * 1024 * 1024, transcendentals=rows * chans
        ),
        name="conv_silu_grads",
    )(video, weights.reshape(9, 3 * chans, chans), cotangent)
    if not reduce_here:
        kgrad = lax.psum_scatter(kgrad, "rows", scatter_dimension=0, tiled=True)
        kgrad = lax.psum_scatter(kgrad, "tm", scatter_dimension=1, tiled=True)
        return activated, input_grad, kgrad
    results = (activated, input_grad, kgrad)
    return pl.pallas_call(
        deliver,
        out_shape=tuple(jax.ShapeDtypeStruct(x.shape, x.dtype) for x in results),
        in_specs=[pl.BlockSpec(memory_space=pltpu.VMEM)] * 3,
        out_specs=(far,) * 3,
        scratch_shapes=[pltpu.SemaphoreType.DMA((3,))],
        compiler_params=pltpu.CompilerParams(vmem_limit_bytes=4 * 1024 * 1024),
        name="deliver",
    )(*results)


def solution(mesh):
    split = P("tm", "rows", None, None)
    return jax.shard_map(
        functools.partial(local, mesh.shape["tm"], mesh.shape["rows"]),
        mesh=mesh,
        in_specs=(split, P(), split),
        out_specs=(split, split, P("rows", "tm")),
        check_vma=False,
    )
```

```python
import functools

import jax
import jax.numpy as jnp
from jax import lax
from jax.experimental import pallas as pl
from jax.experimental.pallas import tpu as pltpu
from jax.sharding import PartitionSpec as P

MESH = pl.DeviceIdType.MESH
F32 = jnp.float32
BF16 = jnp.bfloat16
VMEM_BYTES = (53 * 1024 + 576) * 1024


def along_width(lines, width):
    count, _, chans = lines.shape
    flat = lines.reshape(count * width, chans).astype(F32)
    column = lax.broadcasted_iota(jnp.int32, (count, width, chans), 1).reshape(flat.shape)
    before = jnp.where(column == 0, 0.0, pltpu.roll(flat, 1, 0)).astype(BF16)
    after = jnp.where(column == width - 1, 0.0, pltpu.roll(flat, count * width - 1, 0)).astype(BF16)
    return (
        before.reshape(lines.shape),
        lines,
        after.reshape(lines.shape),
    )


def kernel(
    nt, nr, reduce_here,
    video, weights, cot, act, igrad, kgrad,
    taps, cot_own, seen, patches, gext, gpatches, total, chunks,
    s0, r0, s1a, r1a, s1b, r1b, s2a, r2a, s2b, r2b, a3, s3, r3,
    local_sem, vsend, vrecv, gsend, grecv, ksend, krecv,
):
    frames, height, width, chans = video.shape
    rows = frames * height * width
    tm = lax.axis_index("tm")
    row = lax.axis_index("rows")

    def inside(dt, dr):
        return (tm + dt >= 0) & (tm + dt < nt) & (row + dr >= 0) & (row + dr < nr)

    def wrapped(dt, dr):
        return (lax.rem(tm + dt + nt, nt), lax.rem(row + dr + nr, nr))

    own, top, bottom = pl.ds(1, height), 0, height + 1
    old, new = pl.ds(0, 2), pl.ds(2, frames)
    loads = [
        pltpu.make_async_copy(video, seen.at[new, own], local_sem.at[0]),
        pltpu.make_async_copy(weights, taps, local_sem.at[1]),
        pltpu.make_async_copy(cot, cot_own, local_sem.at[2]),
    ]
    for load in loads:
        load.start()

    barrier = pltpu.get_barrier_semaphore()
    around = [(dt, dr) for dt in (-1, 0, 1) for dr in (-1, 0, 1) if dt or dr]
    expected = 0
    for dt, dr in around:
        greets = copies_to = inside(dt, dr)
        if dt and dr:
            greets = greets & (dt == -1)
            copies_to = copies_to & (dt == 1)
        expected = expected + jnp.where(copies_to, 1, 0)

        @pl.when(greets)
        def _(dt=dt, dr=dr):
            pl.semaphore_signal(barrier, inc=1, device_id=wrapped(dt, dr), device_id_type=MESH)

    if reduce_here:
        depth = lax.div(row, 2)
        side = lax.rem(row, 2)
        across = lax.div(tm, 2)
        core = lax.rem(tm, 2)
        other_core = (across * 2 + 1 - core, row)
        other_across = ((1 - across) * 2 + core, row)
        other_side = (tm, depth * 2 + 1 - side)
        layers = [lax.rem(depth + k, 4) for k in range(4)]
        partners = [other_across] + [(tm, layers[k] * 2 + side) for k in (1, 2, 3)]
        for partner in partners:
            pl.semaphore_signal(barrier, inc=1, device_id=partner, device_id_type=MESH)
        expected = expected + len(partners)
    pl.semaphore_wait(barrier, expected)

    def piece(dt, dr, send_when, source, target, sems, k):
        copy = pltpu.make_async_remote_copy(
            src_ref=source, dst_ref=target,
            send_sem=sems[0].at[k], recv_sem=sems[1].at[k],
            device_id=wrapped(dt, dr), device_id_type=MESH,
        )
        return (copy, send_when)

    def start(part):
        pl.when(part[1])(part[0].start)

    def sent(part):
        pl.when(part[1])(part[0].wait_send)

    def arrive(part, dt, dr, target):
        there = inside(dt, dr)
        pl.when(there)(part[0].wait_recv)

        @pl.when(jnp.logical_not(there))
        def _():
            target[...] = jnp.zeros(target.shape, BF16)

    last = pl.ds(frames - 2, 2)
    vsems, gsems = (vsend, vrecv), (gsend, grecv)
    halo = [
        piece(1, 0, inside(1, 0), video.at[last], seen.at[old, own], vsems, 0),
        piece(0, 1, inside(0, 1), video.at[:, height - 1], seen.at[new, top], vsems, 1),
        piece(0, -1, inside(0, -1), video.at[:, 0], seen.at[new, bottom], vsems, 2),
        piece(1, 1, inside(1, 1), video.at[last, height - 1], seen.at[old, top], vsems, 3),
        piece(1, -1, inside(1, -1), video.at[last, 0], seen.at[old, bottom], vsems, 4),
    ]
    for part in halo:
        start(part)

    def spread(target, fr, ro, lines):
        flat = lines.reshape((-1,) + lines.shape[-2:])
        for c, piece in enumerate(along_width(flat, width)):
            target[fr, ro, :, c * chans:(c + 1) * chans] = piece.reshape(lines.shape)

    def patch(source, a, b):
        return source[a:a + frames, b:b + height].reshape(rows, 3 * chans)

    def forward(a, b):
        return jnp.dot(patch(patches, a, b), taps[a * 3 + b], preferred_element_type=F32)

    loads[0].wait()
    spread(patches, new, own, seen[new, own])
    loads[1].wait()
    pre = forward(2, 1)
    arrive(halo[0], -1, 0, seen.at[old, own])
    spread(patches, old, own, seen[old, own])
    pre = pre + forward(0, 1)
    pre = pre + forward(1, 1)
    arrive(halo[1], 0, -1, seen.at[new, top])
    arrive(halo[2], 0, 1, seen.at[new, bottom])
    spread(patches, new, top, seen[new, top])
    spread(patches, new, bottom, seen[new, bottom])
    pre = pre + forward(2, 0)
    pre = pre + forward(2, 2)
    arrive(halo[3], -1, -1, seen.at[old, top])
    spread(patches, old, top, seen[old, top])
    arrive(halo[4], -1, 1, seen.at[old, bottom])
    spread(patches, old, bottom, seen[old, bottom])
    for b in (0, 2):
        for a in range(2):
            pre = pre + forward(a, b)

    sig = 1.0 / (1.0 + jnp.exp(-pre))
    act[...] = (pre * sig).astype(BF16).reshape(act.shape)
    loads[2].wait()
    cot_flat = cot_own[...].reshape(rows, chans).astype(F32)
    grad = (cot_flat * sig * (1.0 + pre * (1.0 - sig))).astype(BF16)
    mine, later = pl.ds(0, frames), pl.ds(frames, 2)
    early = pl.ds(0, 2)
    gext[mine, own] = grad.reshape(video.shape)
    ghalo = [
        piece(-1, 0, inside(-1, 0), gext.at[early, own], gext.at[later, own], gsems, 0),
        piece(0, 1, inside(0, 1), gext.at[mine, height], gext.at[mine, top], gsems, 1),
        piece(0, -1, inside(0, -1), gext.at[mine, 1], gext.at[mine, bottom], gsems, 2),
        piece(-1, 0, inside(-1, -1), gext.at[early, top], gext.at[later, top], gsems, 3),
        piece(-1, 0, inside(-1, 1), gext.at[early, bottom], gext.at[later, bottom], gsems, 4),
    ]
    for part in ghalo[:3]:
        start(part)

    turned = grad.astype(F32).T.astype(BF16)
    kdepth = 3 * chans

    def weight_part(k):
        total[:, k * kdepth:(k + 1) * kdepth] = jnp.dot(
            turned, patch(patches, k // 3, k % 3), preferred_element_type=F32
        )

    def backward(a, b):
        block = taps.at[(2 - a) * 3 + 2 - b]
        mat = jnp.concatenate(
            [block[(2 - c) * chans:(3 - c) * chans, :] for c in range(3)], axis=1
        )
        return lax.dot_general(
            patch(gpatches, a, b), mat, (((1,), (1,)), ((), ())), preferred_element_type=F32
        )

    def grad_own():
        spread(gpatches, mine, own, grad.reshape(video.shape))
        return backward(0, 1)

    def grad_later(out):
        arrive(ghalo[0], 1, 0, gext.at[later, own])
        spread(gpatches, later, own, gext[later, own])
        return out + backward(1, 1) + backward(2, 1)

    def grad_rows():
        arrive(ghalo[1], 0, -1, gext.at[mine, top])
        start(ghalo[3])
        arrive(ghalo[2], 0, 1, gext.at[mine, bottom])
        start(ghalo[4])

    def grad_edges(out):
        for ro in (top, bottom):
            spread(gpatches, mine, ro, gext[mine, ro])
        return out + backward(0, 0) + backward(0, 2)

    def grad_corners(out):
        arrive(ghalo[3], 1, -1, gext.at[later, top])
        spread(gpatches, later, top, gext[later, top])
        out = out + backward(1, 0) + backward(2, 0)
        arrive(ghalo[4], 1, 1, gext.at[later, bottom])
        spread(gpatches, later, bottom, gext[later, bottom])
        out = out + backward(1, 2) + backward(2, 2)
        igrad[...] = out.astype(BF16).reshape(igrad.shape)

    def finish():
        for part in halo + ghalo:
            sent(part)

    if not reduce_here:
        for k in range(9):
            weight_part(k)
        kgrad[...] = total[...]
        out = grad_later(grad_own())
        grad_rows()
        grad_corners(grad_edges(out))
        finish()
        return

    columns = total.shape[1] // nt
    wide = chunks.shape[-1]

    def cut(j):
        start = columns * j // 128 * 128
        shift = columns * j - start
        span = -(-(shift + columns) // 128) * 128
        piece = total[:, start:start + span]
        if shift:
            piece = pltpu.roll(piece, span - shift, 1)
        chunks[j] = piece[:, :wide].reshape(chunks.shape[1:])

    def send(k, source, target, device):
        copy = pltpu.make_async_remote_copy(
            src_ref=source, dst_ref=target,
            send_sem=ksend.at[k], recv_sem=krecv.at[k],
            device_id=device, device_id_type=MESH,
        )
        copy.start()
        return copy

    halves = [
        pltpu.make_async_remote_copy(
            src_ref=s0.at[half], dst_ref=r0.at[half],
            send_sem=ksend.at[half], recv_sem=krecv.at[half],
            device_id=other_core, device_id_type=MESH,
        )
        for half in range(2)
    ]
    copies = list(halves)
    done = 0
    for j in range(nt):
        need = -(-columns * (j + 1) // kdepth)
        for k in range(done, need):
            weight_part(k)
        done = need
        cut(j)

        @pl.when(core != j % 2)
        def _(j=j):
            s0[j // 2] = chunks[j].astype(BF16)
            halves[j // 2].start()

    out = grad_own()

    near, away = across * 2 + core, (1 - across) * 2 + core
    for half in halves:
        half.wait_recv()
    s1a[...] = (chunks[away, 0:2] + r0[1 - across, 0:2].astype(F32)).astype(BF16)
    copies.append(send(2, s1a, r1a, other_across))
    for half in range(2):
        s1b[half] = (
            chunks[half * 2 + core, 2:4, 1 - side] + r0[half, 2:4, 1 - side].astype(F32)
        ).astype(BF16)
    copies.append(send(3, s1b, r1b, other_side))

    grad_rows()
    out = grad_later(out)

    copies[2].wait_recv()
    s2a[...] = (
        chunks[near, 0:2, 1 - side] + r0[across, 0:2, 1 - side].astype(F32)
        + r1a[:, 1 - side].astype(F32)
    ).astype(BF16)
    copies.append(send(4, s2a, r2a, other_side))
    copies[3].wait_recv()
    s2b[...] = (
        chunks[away, 2:4, side] + r0[1 - across, 2:4, side].astype(F32)
        + r1b[1 - across].astype(F32)
    ).astype(BF16)
    copies.append(send(5, s2b, r2b, other_across))
    a3[0:2] = (
        chunks[near, 0:2, side] + r0[across, 0:2, side].astype(F32) + r1a[:, side].astype(F32)
    )
    a3[2:4] = (
        chunks[near, 2:4, side] + r0[across, 2:4, side].astype(F32) + r1b[across].astype(F32)
    )

    out = grad_edges(out)

    copies[4].wait_recv()
    a3[0:2] = a3[0:2] + r2a[...].astype(F32)
    copies[5].wait_recv()
    a3[2:4] = a3[2:4] + r2b[...].astype(F32)
    for k in (1, 2, 3):
        s3[k - 1] = a3[layers[k]].astype(BF16)
        copies.append(
            send(5 + k, s3.at[k - 1], r3.at[k - 1], (tm, layers[k] * 2 + side))
        )

    grad_corners(out)

    owned = a3[depth]
    for k in (1, 2, 3):
        copies[5 + k].wait_recv()
        owned = owned + r3[k - 1].astype(F32)
    kgrad[...] = owned[:, :columns]
    for copy in copies:
        copy.wait_send()
    finish()


def deliver(*refs):
    count = (len(refs) - 1) // 2
    copies = [pltpu.make_async_copy(refs[k], refs[count + k], refs[-1].at[k]) for k in range(count)]
    for copy in copies:
        copy.start()
    for copy in copies:
        copy.wait()


def local(nt, nr, video, weights, cotangent):
    frames, height, width, chans = video.shape
    rows = frames * height * width
    cols = 27 * chans
    share, columns = chans // nr, cols // nt
    reduce_here = nt == 4 and nr == 8 and share % 16 == 0
    wide = -(-columns // 128) * 128 if reduce_here else 128
    sh = share if reduce_here else 16
    vm = pltpu.VMEM
    far = pl.BlockSpec(memory_space=pl.ANY)
    kshape = (share, columns) if reduce_here else (chans, cols)
    scratch = [
        vm((9, 3 * chans, chans), BF16),
        vm(video.shape, BF16),
        vm((frames + 2, height + 2, width, chans), BF16),
        vm((frames + 2, height + 2, width, 3 * chans), BF16),
        vm((frames + 2, height + 2, width, chans), BF16),
        vm((frames + 2, height + 2, width, 3 * chans), BF16),
        vm((chans, cols), F32),
        vm((4, 4, 2, sh, wide), F32),
        vm((2, 4, 2, sh, wide), BF16),
        vm((2, 4, 2, sh, wide), BF16),
        vm((2, 2, sh, wide), BF16),
        vm((2, 2, sh, wide), BF16),
        vm((2, 2, sh, wide), BF16),
        vm((2, 2, sh, wide), BF16),
        vm((2, sh, wide), BF16),
        vm((2, sh, wide), BF16),
        vm((2, sh, wide), BF16),
        vm((2, sh, wide), BF16),
        vm((4, sh, wide), F32),
        vm((3, sh, wide), BF16),
        vm((3, sh, wide), BF16),
        pltpu.SemaphoreType.DMA((3,)),
        pltpu.SemaphoreType.DMA((5,)),
        pltpu.SemaphoreType.DMA((5,)),
        pltpu.SemaphoreType.DMA((5,)),
        pltpu.SemaphoreType.DMA((5,)),
        pltpu.SemaphoreType.DMA((9,)),
        pltpu.SemaphoreType.DMA((9,)),
    ]
    activated, input_grad, kgrad = pl.pallas_call(
        functools.partial(kernel, nt, nr, reduce_here),
        out_shape=(
            jax.ShapeDtypeStruct(video.shape, BF16),
            jax.ShapeDtypeStruct(video.shape, BF16),
            jax.ShapeDtypeStruct(kshape, F32),
        ),
        in_specs=[far, far, far],
        out_specs=(pl.BlockSpec(memory_space=pltpu.VMEM),) * 3,
        scratch_shapes=scratch,
        compiler_params=pltpu.CompilerParams(
            collective_id=0, has_side_effects=True, vmem_limit_bytes=VMEM_BYTES
        ),
        cost_estimate=pl.CostEstimate(
            flops=6 * rows * cols * chans, bytes_accessed=4 * 1024 * 1024, transcendentals=rows * chans
        ),
        name="conv_silu_grads",
    )(video, weights.reshape(9, 3 * chans, chans), cotangent)
    if not reduce_here:
        kgrad = lax.psum_scatter(kgrad, "rows", scatter_dimension=0, tiled=True)
        kgrad = lax.psum_scatter(kgrad, "tm", scatter_dimension=1, tiled=True)
        return activated, input_grad, kgrad
    results = (activated, input_grad, kgrad)
    return pl.pallas_call(
        deliver,
        out_shape=tuple(jax.ShapeDtypeStruct(x.shape, x.dtype) for x in results),
        in_specs=[pl.BlockSpec(memory_space=pltpu.VMEM)] * 3,
        out_specs=(far,) * 3,
        scratch_shapes=[pltpu.SemaphoreType.DMA((3,))],
        compiler_params=pltpu.CompilerParams(vmem_limit_bytes=4 * 1024 * 1024),
        name="deliver",
    )(*results)


def solution(mesh):
    split = P("tm", "rows", None, None)
    return jax.shard_map(
        functools.partial(local, mesh.shape["tm"], mesh.shape["rows"]),
        mesh=mesh,
        in_specs=(split, P(), split),
        out_specs=(split, split, P("rows", "tm")),
        check_vma=False,
    )
```

```python
import functools

import jax
import jax.numpy as jnp
from jax import lax
from jax.experimental import pallas as pl
from jax.experimental.pallas import tpu as pltpu
from jax.sharding import PartitionSpec as P

MESH = pl.DeviceIdType.MESH
F32 = jnp.float32
BF16 = jnp.bfloat16
VMEM_BYTES = (53 * 1024 + 576) * 1024


def along_width(lines, width):
    count, _, chans = lines.shape
    flat = lines.reshape(count * width, chans).astype(F32)
    column = lax.broadcasted_iota(jnp.int32, (count, width, chans), 1).reshape(flat.shape)
    before = jnp.where(column == 0, 0.0, pltpu.roll(flat, 1, 0)).astype(BF16)
    after = jnp.where(column == width - 1, 0.0, pltpu.roll(flat, count * width - 1, 0)).astype(BF16)
    return (
        before.reshape(lines.shape),
        lines,
        after.reshape(lines.shape),
    )


def kernel(
    nt, nr, reduce_here,
    video, weights, cot, act, igrad, kgrad,
    taps, cot_own, seen, patches, gext, gpatches, total, chunks,
    s0, r0, a1, s1a, r1a, s1b, r1b, a2a, a2b, s2a, r2a, s2b, r2b, a3, s3, r3,
    local_sem, vsend, vrecv, gsend, grecv, ksend, krecv,
):
    frames, height, width, chans = video.shape
    rows = frames * height * width
    tm = lax.axis_index("tm")
    row = lax.axis_index("rows")

    def inside(dt, dr):
        return (tm + dt >= 0) & (tm + dt < nt) & (row + dr >= 0) & (row + dr < nr)

    def wrapped(dt, dr):
        return (lax.rem(tm + dt + nt, nt), lax.rem(row + dr + nr, nr))

    own, top, bottom = pl.ds(1, height), 0, height + 1
    old, new = pl.ds(0, 2), pl.ds(2, frames)
    loads = [
        pltpu.make_async_copy(video, seen.at[new, own], local_sem.at[0]),
        pltpu.make_async_copy(weights, taps, local_sem.at[1]),
        pltpu.make_async_copy(cot, cot_own, local_sem.at[2]),
    ]
    for load in loads:
        load.start()

    barrier = pltpu.get_barrier_semaphore()
    odd = lax.rem(tm, 2) == 1
    around = [(dt, dr) for dt in (-1, 0, 1) for dr in (-1, 0, 1) if dt or dr]
    expected = 0
    for dt, dr in around:
        greets = copies_to = inside(dt, dr)
        if dt and dr:
            greets = greets & (dt == -1) & jnp.logical_not(odd)
            copies_to = copies_to & (dt == 1) & odd
        expected = expected + jnp.where(copies_to, 1, 0)

        @pl.when(greets)
        def _(dt=dt, dr=dr):
            pl.semaphore_signal(barrier, inc=1, device_id=wrapped(dt, dr), device_id_type=MESH)

    if reduce_here:
        depth = lax.div(row, 2)
        side = lax.rem(row, 2)
        across = lax.div(tm, 2)
        core = lax.rem(tm, 2)
        other_core = (across * 2 + 1 - core, row)
        other_across = ((1 - across) * 2 + core, row)
        other_side = (tm, depth * 2 + 1 - side)
        layers = [lax.rem(depth + k, 4) for k in range(4)]
        partners = [other_across] + [(tm, layers[k] * 2 + side) for k in (1, 2, 3)]
        for partner in partners:
            pl.semaphore_signal(barrier, inc=1, device_id=partner, device_id_type=MESH)
        expected = expected + len(partners)
    pl.semaphore_wait(barrier, expected)

    def piece(dt, dr, send_when, source, target, sems, k):
        copy = pltpu.make_async_remote_copy(
            src_ref=source, dst_ref=target,
            send_sem=sems[0].at[k], recv_sem=sems[1].at[k],
            device_id=wrapped(dt, dr), device_id_type=MESH,
        )
        return (copy, send_when)

    def start(part, also=True):
        pl.when(part[1] & also)(part[0].start)

    def sent(part):
        pl.when(part[1])(part[0].wait_send)

    def arrive(part, dt, dr, target):
        there = inside(dt, dr)
        pl.when(there)(part[0].wait_recv)

        @pl.when(jnp.logical_not(there))
        def _():
            target[...] = jnp.zeros(target.shape, BF16)

    last = pl.ds(frames - 2, 2)
    vsems, gsems = (vsend, vrecv), (gsend, grecv)
    halo = [
        piece(1, 0, inside(1, 0), video.at[last], seen.at[old, own], vsems, 0),
        piece(0, 1, inside(0, 1), video.at[:, height - 1], seen.at[new, top], vsems, 1),
        piece(0, -1, inside(0, -1), video.at[:, 0], seen.at[new, bottom], vsems, 2),
        piece(1, 1, inside(1, 1) & odd, video.at[last, height - 1], seen.at[old, top], vsems, 3),
        piece(1, -1, inside(1, -1) & odd, video.at[last, 0], seen.at[old, bottom], vsems, 4),
    ]
    for part in halo:
        start(part)
    even = jnp.logical_not(odd)
    newest = pl.ds(frames, 2)
    passed = [
        piece(1, 0, inside(1, -1) & even, seen.at[newest, top], seen.at[old, top], vsems, 3),
        piece(1, 0, inside(1, 1) & even, seen.at[newest, bottom], seen.at[old, bottom], vsems, 4),
    ]

    def spread(target, fr, ro, lines):
        flat = lines.reshape((-1,) + lines.shape[-2:])
        for c, piece in enumerate(along_width(flat, width)):
            target[fr, ro, :, c * chans:(c + 1) * chans] = piece.reshape(lines.shape)

    def patch(source, a, b):
        return source[a:a + frames, b:b + height].reshape(rows, 3 * chans)

    def forward(a, b):
        return jnp.dot(patch(patches, a, b), taps[a * 3 + b], preferred_element_type=F32)

    loads[0].wait()
    spread(patches, new, own, seen[new, own])
    loads[1].wait()
    pre = forward(2, 1)
    arrive(halo[0], -1, 0, seen.at[old, own])
    spread(patches, old, own, seen[old, own])
    pre = pre + forward(0, 1)
    pre = pre + forward(1, 1)
    arrive(halo[1], 0, -1, seen.at[new, top])
    start(passed[0])
    arrive(halo[2], 0, 1, seen.at[new, bottom])
    start(passed[1])
    spread(patches, new, top, seen[new, top])
    spread(patches, new, bottom, seen[new, bottom])
    pre = pre + forward(2, 0)
    pre = pre + forward(2, 2)
    arrive(halo[3], -1, -1, seen.at[old, top])
    spread(patches, old, top, seen[old, top])
    arrive(halo[4], -1, 1, seen.at[old, bottom])
    spread(patches, old, bottom, seen[old, bottom])
    for b in (0, 2):
        for a in range(2):
            pre = pre + forward(a, b)

    sig = 1.0 / (1.0 + jnp.exp(-pre))
    act[...] = (pre * sig).astype(BF16).reshape(act.shape)
    loads[2].wait()
    cot_flat = cot_own[...].reshape(rows, chans).astype(F32)
    grad = (cot_flat * sig * (1.0 + pre * (1.0 - sig))).astype(BF16)
    mine, later = pl.ds(0, frames), pl.ds(frames, 2)
    early = pl.ds(0, 2)
    gext[mine, own] = grad.reshape(video.shape)
    ghalo = [
        piece(-1, 0, inside(-1, 0), gext.at[early, own], gext.at[later, own], gsems, 0),
        piece(0, 1, inside(0, 1), gext.at[mine, height], gext.at[mine, top], gsems, 1),
        piece(0, -1, inside(0, -1), gext.at[mine, 1], gext.at[mine, bottom], gsems, 2),
        piece(-1, 0, inside(-1, -1), gext.at[early, top], gext.at[later, top], gsems, 3),
        piece(-1, 0, inside(-1, 1), gext.at[early, bottom], gext.at[later, bottom], gsems, 4),
    ]
    start(ghalo[0], even if reduce_here else True)
    start(ghalo[1])
    start(ghalo[2])

    turned = grad.astype(F32).T.astype(BF16)
    kdepth = 3 * chans

    def weight_part(k):
        total[:, k * kdepth:(k + 1) * kdepth] = jnp.dot(
            turned, patch(patches, k // 3, k % 3), preferred_element_type=F32
        )

    def backward(a, b):
        block = taps.at[(2 - a) * 3 + 2 - b]
        mat = jnp.concatenate(
            [block[(2 - c) * chans:(3 - c) * chans, :] for c in range(3)], axis=1
        )
        return lax.dot_general(
            patch(gpatches, a, b), mat, (((1,), (1,)), ((), ())), preferred_element_type=F32
        )

    def grad_own():
        spread(gpatches, mine, own, grad.reshape(video.shape))
        return backward(0, 1)

    def grad_later(out):
        arrive(ghalo[0], 1, 0, gext.at[later, own])
        spread(gpatches, later, own, gext[later, own])
        return out + backward(1, 1) + backward(2, 1)

    def grad_rows():
        arrive(ghalo[1], 0, -1, gext.at[mine, top])
        start(ghalo[3])
        arrive(ghalo[2], 0, 1, gext.at[mine, bottom])
        start(ghalo[4])

    def grad_edges(out):
        for ro in (top, bottom):
            spread(gpatches, mine, ro, gext[mine, ro])
        return out + backward(0, 0) + backward(0, 2)

    def grad_corners(out):
        arrive(ghalo[3], 1, -1, gext.at[later, top])
        spread(gpatches, later, top, gext[later, top])
        out = out + backward(1, 0) + backward(2, 0)
        arrive(ghalo[4], 1, 1, gext.at[later, bottom])
        spread(gpatches, later, bottom, gext[later, bottom])
        out = out + backward(1, 2) + backward(2, 2)
        igrad[...] = out.astype(BF16).reshape(igrad.shape)

    def finish():
        for part in halo + passed + ghalo:
            sent(part)

    if not reduce_here:
        for k in range(9):
            weight_part(k)
        kgrad[...] = total[...]
        out = grad_later(grad_own())
        grad_rows()
        grad_corners(grad_edges(out))
        finish()
        return

    columns = total.shape[1] // nt
    wide = chunks.shape[-1]

    def cut(j):
        start = columns * j // 128 * 128
        shift = columns * j - start
        span = -(-(shift + columns) // 128) * 128
        piece = total[:, start:start + span]
        if shift:
            piece = pltpu.roll(piece, span - shift, 1)
        chunks[j] = piece[:, :wide].reshape(chunks.shape[1:])

    def send(k, source, target, device):
        copy = pltpu.make_async_remote_copy(
            src_ref=source, dst_ref=target,
            send_sem=ksend.at[k], recv_sem=krecv.at[k],
            device_id=device, device_id_type=MESH,
        )
        copy.start()
        return copy

    copies = []
    done = 0
    for half in range(2):
        need = -(-columns * (2 * half + 2) // kdepth)
        for k in range(done, need):
            weight_part(k)
        done = need
        cut(2 * half)
        cut(2 * half + 1)
        s0[half] = chunks[2 * half + 1 - core].astype(BF16)
        copies.append(send(half, s0.at[half], r0.at[half], other_core))

    out = grad_own()

    for half in range(2):
        copies[half].wait_recv()
        a1[half] = chunks[2 * half + core] + r0[half].astype(F32)
    s1a[...] = a1[1 - across, 0:2].astype(BF16)
    copies.append(send(2, s1a, r1a, other_across))
    s1b[...] = a1[:, 2:4, 1 - side].astype(BF16)
    copies.append(send(3, s1b, r1b, other_side))

    start(ghalo[0], odd)
    grad_rows()
    out = grad_edges(out)

    copies[2].wait_recv()
    a2a[...] = a1[across, 0:2] + r1a[...].astype(F32)
    s2a[...] = a2a[:, 1 - side].astype(BF16)
    copies.append(send(4, s2a, r2a, other_side))
    copies[3].wait_recv()
    a2b[...] = a1[:, 2:4, side] + r1b[...].astype(F32)
    s2b[...] = a2b[1 - across].astype(BF16)
    copies.append(send(5, s2b, r2b, other_across))

    out = grad_later(out)

    copies[4].wait_recv()
    a3[0:2] = a2a[:, side] + r2a[...].astype(F32)
    copies[5].wait_recv()
    a3[2:4] = a2b[across] + r2b[...].astype(F32)
    for k in (1, 2, 3):
        s3[k - 1] = a3[layers[k]].astype(BF16)
        copies.append(
            send(5 + k, s3.at[k - 1], r3.at[k - 1], (tm, layers[k] * 2 + side))
        )

    grad_corners(out)

    owned = a3[depth]
    for k in (1, 2, 3):
        copies[5 + k].wait_recv()
        owned = owned + r3[k - 1].astype(F32)
    kgrad[...] = owned[:, :columns]
    for copy in copies:
        copy.wait_send()
    finish()


def deliver(*refs):
    count = (len(refs) - 1) // 2
    copies = [pltpu.make_async_copy(refs[k], refs[count + k], refs[-1].at[k]) for k in range(count)]
    for copy in copies:
        copy.start()
    for copy in copies:
        copy.wait()


def local(nt, nr, video, weights, cotangent):
    frames, height, width, chans = video.shape
    rows = frames * height * width
    cols = 27 * chans
    share, columns = chans // nr, cols // nt
    reduce_here = nt == 4 and nr == 8 and share % 16 == 0
    wide = -(-columns // 128) * 128 if reduce_here else 128
    sh = share if reduce_here else 16
    vm = pltpu.VMEM
    far = pl.BlockSpec(memory_space=pl.ANY)
    kshape = (share, columns) if reduce_here else (chans, cols)
    scratch = [
        vm((9, 3 * chans, chans), BF16),
        vm(video.shape, BF16),
        vm((frames + 2, height + 2, width, chans), BF16),
        vm((frames + 2, height + 2, width, 3 * chans), BF16),
        vm((frames + 2, height + 2, width, chans), BF16),
        vm((frames + 2, height + 2, width, 3 * chans), BF16),
        vm((chans, cols), F32),
        vm((4, 4, 2, sh, wide), F32),
        vm((2, 4, 2, sh, wide), BF16),
        vm((2, 4, 2, sh, wide), BF16),
        vm((2, 4, 2, sh, wide), F32),
        vm((2, 2, sh, wide), BF16),
        vm((2, 2, sh, wide), BF16),
        vm((2, 2, sh, wide), BF16),
        vm((2, 2, sh, wide), BF16),
        vm((2, 2, sh, wide), F32),
        vm((2, 2, sh, wide), F32),
        vm((2, sh, wide), BF16),
        vm((2, sh, wide), BF16),
        vm((2, sh, wide), BF16),
        vm((2, sh, wide), BF16),
        vm((4, sh, wide), F32),
        vm((3, sh, wide), BF16),
        vm((3, sh, wide), BF16),
        pltpu.SemaphoreType.DMA((3,)),
        pltpu.SemaphoreType.DMA((5,)),
        pltpu.SemaphoreType.DMA((5,)),
        pltpu.SemaphoreType.DMA((5,)),
        pltpu.SemaphoreType.DMA((5,)),
        pltpu.SemaphoreType.DMA((9,)),
        pltpu.SemaphoreType.DMA((9,)),
    ]
    activated, input_grad, kgrad = pl.pallas_call(
        functools.partial(kernel, nt, nr, reduce_here),
        out_shape=(
            jax.ShapeDtypeStruct(video.shape, BF16),
            jax.ShapeDtypeStruct(video.shape, BF16),
            jax.ShapeDtypeStruct(kshape, F32),
        ),
        in_specs=[far, far, far],
        out_specs=(pl.BlockSpec(memory_space=pltpu.VMEM),) * 3,
        scratch_shapes=scratch,
        compiler_params=pltpu.CompilerParams(
            collective_id=0, has_side_effects=True, vmem_limit_bytes=VMEM_BYTES
        ),
        cost_estimate=pl.CostEstimate(
            flops=6 * rows * cols * chans, bytes_accessed=4 * 1024 * 1024, transcendentals=rows * chans
        ),
        name="conv_silu_grads",
    )(video, weights.reshape(9, 3 * chans, chans), cotangent)
    if not reduce_here:
        kgrad = lax.psum_scatter(kgrad, "rows", scatter_dimension=0, tiled=True)
        kgrad = lax.psum_scatter(kgrad, "tm", scatter_dimension=1, tiled=True)
        return activated, input_grad, kgrad
    results = (activated, input_grad, kgrad)
    return pl.pallas_call(
        deliver,
        out_shape=tuple(jax.ShapeDtypeStruct(x.shape, x.dtype) for x in results),
        in_specs=[pl.BlockSpec(memory_space=pltpu.VMEM)] * 3,
        out_specs=(far,) * 3,
        scratch_shapes=[pltpu.SemaphoreType.DMA((3,))],
        compiler_params=pltpu.CompilerParams(vmem_limit_bytes=4 * 1024 * 1024),
        name="deliver",
    )(*results)


def solution(mesh):
    split = P("tm", "rows", None, None)
    return jax.shard_map(
        functools.partial(local, mesh.shape["tm"], mesh.shape["rows"]),
        mesh=mesh,
        in_specs=(split, P(), split),
        out_specs=(split, split, P("rows", "tm")),
        check_vma=False,
    )
```

```python
import functools

import jax
import jax.numpy as jnp
from jax import lax
from jax.experimental import pallas as pl
from jax.experimental.pallas import tpu as pltpu
from jax.sharding import PartitionSpec as P

MESH = pl.DeviceIdType.MESH
F32 = jnp.float32
BF16 = jnp.bfloat16
VMEM_BYTES = (53 * 1024 + 576) * 1024


def along_width(lines, width):
    count, _, chans = lines.shape
    flat = lines.reshape(count * width, chans).astype(F32)
    column = lax.broadcasted_iota(jnp.int32, (count, width, chans), 1).reshape(flat.shape)
    before = jnp.where(column == 0, 0.0, pltpu.roll(flat, 1, 0)).astype(BF16)
    after = jnp.where(column == width - 1, 0.0, pltpu.roll(flat, count * width - 1, 0)).astype(BF16)
    return (
        before.reshape(lines.shape),
        lines,
        after.reshape(lines.shape),
    )


def kernel(
    nt, nr, reduce_here,
    video, weights, cot, act, igrad, kgrad,
    taps, cot_own, seen, patches, gext, gpatches, total, chunks,
    s0, r0, s1a, r1a, s1b, r1b, s2a, r2a, s2b, r2b, a3, s3, r3,
    local_sem, vsend, vrecv, gsend, grecv, ksend, krecv,
):
    frames, height, width, chans = video.shape
    rows = frames * height * width
    tm = lax.axis_index("tm")
    row = lax.axis_index("rows")

    def inside(dt, dr):
        return (tm + dt >= 0) & (tm + dt < nt) & (row + dr >= 0) & (row + dr < nr)

    def wrapped(dt, dr):
        return (lax.rem(tm + dt + nt, nt), lax.rem(row + dr + nr, nr))

    own, top, bottom = pl.ds(1, height), 0, height + 1
    old, new = pl.ds(0, 2), pl.ds(2, frames)
    loads = [
        pltpu.make_async_copy(video, seen.at[new, own], local_sem.at[0]),
        pltpu.make_async_copy(weights, taps, local_sem.at[1]),
        pltpu.make_async_copy(cot, cot_own, local_sem.at[2]),
    ]
    for load in loads:
        load.start()

    barrier = pltpu.get_barrier_semaphore()
    odd = lax.rem(tm, 2) == 1
    around = [(dt, dr) for dt in (-1, 0, 1) for dr in (-1, 0, 1) if dt or dr]
    expected = 0
    for dt, dr in around:
        greets = copies_to = inside(dt, dr)
        if dt and dr:
            greets = greets & (dt == -1) & jnp.logical_not(odd)
            copies_to = copies_to & (dt == 1) & odd
        expected = expected + jnp.where(copies_to, 1, 0)

        @pl.when(greets)
        def _(dt=dt, dr=dr):
            pl.semaphore_signal(barrier, inc=1, device_id=wrapped(dt, dr), device_id_type=MESH)

    if reduce_here:
        depth = lax.div(row, 2)
        side = lax.rem(row, 2)
        across = lax.div(tm, 2)
        core = lax.rem(tm, 2)
        other_core = (across * 2 + 1 - core, row)
        other_across = ((1 - across) * 2 + core, row)
        other_side = (tm, depth * 2 + 1 - side)
        layers = [lax.rem(depth + k, 4) for k in range(4)]
        partners = [other_across] + [(tm, layers[k] * 2 + side) for k in (1, 2, 3)]
        for partner in partners:
            pl.semaphore_signal(barrier, inc=1, device_id=partner, device_id_type=MESH)
        expected = expected + len(partners)
    pl.semaphore_wait(barrier, expected)

    def piece(dt, dr, send_when, source, target, sems, k):
        copy = pltpu.make_async_remote_copy(
            src_ref=source, dst_ref=target,
            send_sem=sems[0].at[k], recv_sem=sems[1].at[k],
            device_id=wrapped(dt, dr), device_id_type=MESH,
        )
        return (copy, send_when)

    def start(part):
        pl.when(part[1])(part[0].start)

    def sent(part):
        pl.when(part[1])(part[0].wait_send)

    def arrive(part, dt, dr, target):
        there = inside(dt, dr)
        pl.when(there)(part[0].wait_recv)

        @pl.when(jnp.logical_not(there))
        def _():
            target[...] = jnp.zeros(target.shape, BF16)

    last = pl.ds(frames - 2, 2)
    vsems, gsems = (vsend, vrecv), (gsend, grecv)
    halo = [
        piece(1, 0, inside(1, 0), video.at[last], seen.at[old, own], vsems, 0),
        piece(0, 1, inside(0, 1), video.at[:, height - 1], seen.at[new, top], vsems, 1),
        piece(0, -1, inside(0, -1), video.at[:, 0], seen.at[new, bottom], vsems, 2),
        piece(1, 1, inside(1, 1) & odd, video.at[last, height - 1], seen.at[old, top], vsems, 3),
        piece(1, -1, inside(1, -1) & odd, video.at[last, 0], seen.at[old, bottom], vsems, 4),
    ]
    even = jnp.logical_not(odd)
    for part in halo:
        start(part)
    newest = pl.ds(frames, 2)
    passed = [
        piece(1, 0, inside(1, -1) & even, seen.at[newest, top], seen.at[old, top], vsems, 3),
        piece(1, 0, inside(1, 1) & even, seen.at[newest, bottom], seen.at[old, bottom], vsems, 4),
    ]

    def spread(target, fr, ro, lines):
        flat = lines.reshape((-1,) + lines.shape[-2:])
        for c, piece in enumerate(along_width(flat, width)):
            target[fr, ro, :, c * chans:(c + 1) * chans] = piece.reshape(lines.shape)

    def patch(source, a, b):
        return source[a:a + frames, b:b + height].reshape(rows, 3 * chans)

    def forward(a, b):
        return jnp.dot(patch(patches, a, b), taps[a * 3 + b], preferred_element_type=F32)

    loads[0].wait()
    spread(patches, new, own, seen[new, own])
    loads[1].wait()
    pre = forward(2, 1)
    arrive(halo[0], -1, 0, seen.at[old, own])
    spread(patches, old, own, seen[old, own])
    pre = pre + forward(0, 1)
    pre = pre + forward(1, 1)
    arrive(halo[1], 0, -1, seen.at[new, top])
    start(passed[0])
    arrive(halo[2], 0, 1, seen.at[new, bottom])
    start(passed[1])
    spread(patches, new, top, seen[new, top])
    spread(patches, new, bottom, seen[new, bottom])
    pre = pre + forward(2, 0)
    pre = pre + forward(2, 2)
    arrive(halo[3], -1, -1, seen.at[old, top])
    spread(patches, old, top, seen[old, top])
    arrive(halo[4], -1, 1, seen.at[old, bottom])
    spread(patches, old, bottom, seen[old, bottom])
    for b in (0, 2):
        for a in range(2):
            pre = pre + forward(a, b)

    sig = 1.0 / (1.0 + jnp.exp(-pre))
    act[...] = (pre * sig).astype(BF16).reshape(act.shape)
    loads[2].wait()
    cot_flat = cot_own[...].reshape(rows, chans).astype(F32)
    grad = (cot_flat * sig * (1.0 + pre * (1.0 - sig))).astype(BF16)
    mine, later = pl.ds(0, frames), pl.ds(frames, 2)
    early = pl.ds(0, 2)
    gext[mine, own] = grad.reshape(video.shape)
    ghalo = [
        piece(-1, 0, inside(-1, 0), gext.at[early, own], gext.at[later, own], gsems, 0),
        piece(0, 1, inside(0, 1), gext.at[mine, height], gext.at[mine, top], gsems, 1),
        piece(0, -1, inside(0, -1), gext.at[mine, 1], gext.at[mine, bottom], gsems, 2),
        piece(-1, 0, inside(-1, -1), gext.at[early, top], gext.at[later, top], gsems, 3),
        piece(-1, 0, inside(-1, 1), gext.at[early, bottom], gext.at[later, bottom], gsems, 4),
    ]
    for part in ghalo[:3]:
        start(part)

    turned = grad.astype(F32).T.astype(BF16)
    kdepth = 3 * chans

    def weight_part(k):
        total[:, k * kdepth:(k + 1) * kdepth] = jnp.dot(
            turned, patch(patches, k // 3, k % 3), preferred_element_type=F32
        )

    def backward(a, b):
        block = taps.at[(2 - a) * 3 + 2 - b]
        mat = jnp.concatenate(
            [block[(2 - c) * chans:(3 - c) * chans, :] for c in range(3)], axis=1
        )
        return lax.dot_general(
            patch(gpatches, a, b), mat, (((1,), (1,)), ((), ())), preferred_element_type=F32
        )

    def grad_own():
        spread(gpatches, mine, own, grad.reshape(video.shape))
        return backward(0, 1)

    def grad_later(out):
        arrive(ghalo[0], 1, 0, gext.at[later, own])
        spread(gpatches, later, own, gext[later, own])
        return out + backward(1, 1) + backward(2, 1)

    def grad_rows():
        arrive(ghalo[1], 0, -1, gext.at[mine, top])
        start(ghalo[3])
        arrive(ghalo[2], 0, 1, gext.at[mine, bottom])
        start(ghalo[4])

    def grad_edges(out):
        for ro in (top, bottom):
            spread(gpatches, mine, ro, gext[mine, ro])
        return out + backward(0, 0) + backward(0, 2)

    def grad_corners(out):
        arrive(ghalo[3], 1, -1, gext.at[later, top])
        spread(gpatches, later, top, gext[later, top])
        out = out + backward(1, 0) + backward(2, 0)
        arrive(ghalo[4], 1, 1, gext.at[later, bottom])
        spread(gpatches, later, bottom, gext[later, bottom])
        out = out + backward(1, 2) + backward(2, 2)
        igrad[...] = out.astype(BF16).reshape(igrad.shape)

    def finish():
        for part in halo + passed + ghalo:
            sent(part)

    if not reduce_here:
        for k in range(9):
            weight_part(k)
        kgrad[...] = total[...]
        out = grad_later(grad_own())
        grad_rows()
        grad_corners(grad_edges(out))
        finish()
        return

    columns = total.shape[1] // nt
    wide = chunks.shape[-1]

    def cut(j):
        start = columns * j // 128 * 128
        shift = columns * j - start
        span = -(-(shift + columns) // 128) * 128
        piece = total[:, start:start + span]
        if shift:
            piece = pltpu.roll(piece, span - shift, 1)
        chunks[j] = piece[:, :wide].reshape(chunks.shape[1:])

    def send(k, source, target, device):
        copy = pltpu.make_async_remote_copy(
            src_ref=source, dst_ref=target,
            send_sem=ksend.at[k], recv_sem=krecv.at[k],
            device_id=device, device_id_type=MESH,
        )
        copy.start()
        return copy

    halves = [
        pltpu.make_async_remote_copy(
            src_ref=s0.at[half], dst_ref=r0.at[half],
            send_sem=ksend.at[half], recv_sem=krecv.at[half],
            device_id=other_core, device_id_type=MESH,
        )
        for half in range(2)
    ]
    copies = list(halves)
    done = 0
    for j in range(nt):
        need = -(-columns * (j + 1) // kdepth)
        for k in range(done, need):
            weight_part(k)
        done = need
        cut(j)

        @pl.when(core != j % 2)
        def _(j=j):
            s0[j // 2] = chunks[j].astype(BF16)
            halves[j // 2].start()

    out = grad_own()

    near, away = across * 2 + core, (1 - across) * 2 + core
    for half in halves:
        half.wait_recv()
    s1a[...] = (chunks[away, 0:2] + r0[1 - across, 0:2].astype(F32)).astype(BF16)
    copies.append(send(2, s1a, r1a, other_across))
    for half in range(2):
        s1b[half] = (
            chunks[half * 2 + core, 2:4, 1 - side] + r0[half, 2:4, 1 - side].astype(F32)
        ).astype(BF16)
    copies.append(send(3, s1b, r1b, other_side))

    grad_rows()
    out = grad_later(out)

    copies[2].wait_recv()
    s2a[...] = (
        chunks[near, 0:2, 1 - side] + r0[across, 0:2, 1 - side].astype(F32)
        + r1a[:, 1 - side].astype(F32)
    ).astype(BF16)
    copies.append(send(4, s2a, r2a, other_side))
    copies[3].wait_recv()
    s2b[...] = (
        chunks[away, 2:4, side] + r0[1 - across, 2:4, side].astype(F32)
        + r1b[1 - across].astype(F32)
    ).astype(BF16)
    copies.append(send(5, s2b, r2b, other_across))
    a3[0:2] = (
        chunks[near, 0:2, side] + r0[across, 0:2, side].astype(F32) + r1a[:, side].astype(F32)
    )
    a3[2:4] = (
        chunks[near, 2:4, side] + r0[across, 2:4, side].astype(F32) + r1b[across].astype(F32)
    )

    out = grad_edges(out)

    copies[4].wait_recv()
    a3[0:2] = a3[0:2] + r2a[...].astype(F32)
    copies[5].wait_recv()
    a3[2:4] = a3[2:4] + r2b[...].astype(F32)
    for k in (1, 2, 3):
        s3[k - 1] = a3[layers[k]].astype(BF16)
        copies.append(
            send(5 + k, s3.at[k - 1], r3.at[k - 1], (tm, layers[k] * 2 + side))
        )

    grad_corners(out)

    owned = a3[depth]
    for k in (1, 2, 3):
        copies[5 + k].wait_recv()
        owned = owned + r3[k - 1].astype(F32)
    kgrad[...] = owned[:, :columns]
    for copy in copies:
        copy.wait_send()
    finish()


def deliver(*refs):
    count = (len(refs) - 1) // 2
    copies = [pltpu.make_async_copy(refs[k], refs[count + k], refs[-1].at[k]) for k in range(count)]
    for copy in copies:
        copy.start()
    for copy in copies:
        copy.wait()


def local(nt, nr, video, weights, cotangent):
    frames, height, width, chans = video.shape
    rows = frames * height * width
    cols = 27 * chans
    share, columns = chans // nr, cols // nt
    reduce_here = nt == 4 and nr == 8 and share % 16 == 0
    wide = -(-columns // 128) * 128 if reduce_here else 128
    sh = share if reduce_here else 16
    vm = pltpu.VMEM
    far = pl.BlockSpec(memory_space=pl.ANY)
    kshape = (share, columns) if reduce_here else (chans, cols)
    scratch = [
        vm((9, 3 * chans, chans), BF16),
        vm(video.shape, BF16),
        vm((frames + 2, height + 2, width, chans), BF16),
        vm((frames + 2, height + 2, width, 3 * chans), BF16),
        vm((frames + 2, height + 2, width, chans), BF16),
        vm((frames + 2, height + 2, width, 3 * chans), BF16),
        vm((chans, cols), F32),
        vm((4, 4, 2, sh, wide), F32),
        vm((2, 4, 2, sh, wide), BF16),
        vm((2, 4, 2, sh, wide), BF16),
        vm((2, 2, sh, wide), BF16),
        vm((2, 2, sh, wide), BF16),
        vm((2, 2, sh, wide), BF16),
        vm((2, 2, sh, wide), BF16),
        vm((2, sh, wide), BF16),
        vm((2, sh, wide), BF16),
        vm((2, sh, wide), BF16),
        vm((2, sh, wide), BF16),
        vm((4, sh, wide), F32),
        vm((3, sh, wide), BF16),
        vm((3, sh, wide), BF16),
        pltpu.SemaphoreType.DMA((3,)),
        pltpu.SemaphoreType.DMA((5,)),
        pltpu.SemaphoreType.DMA((5,)),
        pltpu.SemaphoreType.DMA((5,)),
        pltpu.SemaphoreType.DMA((5,)),
        pltpu.SemaphoreType.DMA((9,)),
        pltpu.SemaphoreType.DMA((9,)),
    ]
    activated, input_grad, kgrad = pl.pallas_call(
        functools.partial(kernel, nt, nr, reduce_here),
        out_shape=(
            jax.ShapeDtypeStruct(video.shape, BF16),
            jax.ShapeDtypeStruct(video.shape, BF16),
            jax.ShapeDtypeStruct(kshape, F32),
        ),
        in_specs=[far, far, far],
        out_specs=(pl.BlockSpec(memory_space=pltpu.VMEM),) * 3,
        scratch_shapes=scratch,
        compiler_params=pltpu.CompilerParams(
            collective_id=0, has_side_effects=True, vmem_limit_bytes=VMEM_BYTES
        ),
        cost_estimate=pl.CostEstimate(
            flops=6 * rows * cols * chans, bytes_accessed=4 * 1024 * 1024, transcendentals=rows * chans
        ),
        name="conv_silu_grads",
    )(video, weights.reshape(9, 3 * chans, chans), cotangent)
    if not reduce_here:
        kgrad = lax.psum_scatter(kgrad, "rows", scatter_dimension=0, tiled=True)
        kgrad = lax.psum_scatter(kgrad, "tm", scatter_dimension=1, tiled=True)
        return activated, input_grad, kgrad
    results = (activated, input_grad, kgrad)
    return pl.pallas_call(
        deliver,
        out_shape=tuple(jax.ShapeDtypeStruct(x.shape, x.dtype) for x in results),
        in_specs=[pl.BlockSpec(memory_space=pltpu.VMEM)] * 3,
        out_specs=(far,) * 3,
        scratch_shapes=[pltpu.SemaphoreType.DMA((3,))],
        compiler_params=pltpu.CompilerParams(vmem_limit_bytes=4 * 1024 * 1024),
        name="deliver",
    )(*results)


def solution(mesh):
    split = P("tm", "rows", None, None)
    return jax.shard_map(
        functools.partial(local, mesh.shape["tm"], mesh.shape["rows"]),
        mesh=mesh,
        in_specs=(split, P(), split),
        out_specs=(split, split, P("rows", "tm")),
        check_vma=False,
    )
```

```python
import functools

import jax
import jax.numpy as jnp
from jax import lax
from jax.experimental import pallas as pl
from jax.experimental.pallas import tpu as pltpu
from jax.sharding import PartitionSpec as P

MESH = pl.DeviceIdType.MESH
F32 = jnp.float32
BF16 = jnp.bfloat16
VMEM_BYTES = (53 * 1024 + 576) * 1024


def along_width(lines, width):
    count, _, chans = lines.shape
    flat = lines.reshape(count * width, chans).astype(F32)
    column = lax.broadcasted_iota(jnp.int32, (count, width, chans), 1).reshape(flat.shape)
    before = jnp.where(column == 0, 0.0, pltpu.roll(flat, 1, 0)).astype(BF16)
    after = jnp.where(column == width - 1, 0.0, pltpu.roll(flat, count * width - 1, 0)).astype(BF16)
    return (
        before.reshape(lines.shape),
        lines,
        after.reshape(lines.shape),
    )


def kernel(
    nt, nr, reduce_here,
    video, weights, cot, act, igrad, kgrad,
    taps, cot_own, seen, patches, gext, gpatches, total, chunks,
    s0, r0, a1, s1a, r1a, s1b, r1b, a2a, a2b, s2a, r2a, s2b, r2b, a3, s3, r3,
    local_sem, vsend, vrecv, gsend, grecv, ksend, krecv,
):
    frames, height, width, chans = video.shape
    rows = frames * height * width
    tm = lax.axis_index("tm")
    row = lax.axis_index("rows")

    def inside(dt, dr):
        return (tm + dt >= 0) & (tm + dt < nt) & (row + dr >= 0) & (row + dr < nr)

    def wrapped(dt, dr):
        return (lax.rem(tm + dt + nt, nt), lax.rem(row + dr + nr, nr))

    own, top, bottom = pl.ds(1, height), 0, height + 1
    old, new = pl.ds(0, 2), pl.ds(2, frames)
    loads = [
        pltpu.make_async_copy(video, seen.at[new, own], local_sem.at[0]),
        pltpu.make_async_copy(weights, taps, local_sem.at[1]),
        pltpu.make_async_copy(cot, cot_own, local_sem.at[2]),
    ]
    for load in loads:
        load.start()

    barrier = pltpu.get_barrier_semaphore()
    odd = lax.rem(tm, 2) == 1
    around = [(dt, dr) for dt in (-1, 0, 1) for dr in (-1, 0, 1) if dt or dr]
    expected = 0
    for dt, dr in around:
        greets = copies_to = inside(dt, dr)
        if dt and dr:
            greets = greets & (dt == -1) & jnp.logical_not(odd)
            copies_to = copies_to & (dt == 1) & odd
        expected = expected + jnp.where(copies_to, 1, 0)

        @pl.when(greets)
        def _(dt=dt, dr=dr):
            pl.semaphore_signal(barrier, inc=1, device_id=wrapped(dt, dr), device_id_type=MESH)

    if reduce_here:
        depth = lax.div(row, 2)
        side = lax.rem(row, 2)
        across = lax.div(tm, 2)
        core = lax.rem(tm, 2)
        other_core = (across * 2 + 1 - core, row)
        other_across = ((1 - across) * 2 + core, row)
        other_side = (tm, depth * 2 + 1 - side)
        layers = [lax.rem(depth + k, 4) for k in range(4)]
        partners = [other_across] + [(tm, layers[k] * 2 + side) for k in (1, 2, 3)]
        for partner in partners:
            pl.semaphore_signal(barrier, inc=1, device_id=partner, device_id_type=MESH)
        expected = expected + len(partners)
    pl.semaphore_wait(barrier, expected)

    def piece(dt, dr, send_when, source, target, sems, k):
        copy = pltpu.make_async_remote_copy(
            src_ref=source, dst_ref=target,
            send_sem=sems[0].at[k], recv_sem=sems[1].at[k],
            device_id=wrapped(dt, dr), device_id_type=MESH,
        )
        return (copy, send_when)

    def start(part):
        pl.when(part[1])(part[0].start)

    def sent(part):
        pl.when(part[1])(part[0].wait_send)

    def arrive(part, dt, dr, target):
        there = inside(dt, dr)
        pl.when(there)(part[0].wait_recv)

        @pl.when(jnp.logical_not(there))
        def _():
            target[...] = jnp.zeros(target.shape, BF16)

    last = pl.ds(frames - 2, 2)
    vsems, gsems = (vsend, vrecv), (gsend, grecv)
    halo = [
        piece(1, 0, inside(1, 0), video.at[last], seen.at[old, own], vsems, 0),
        piece(0, 1, inside(0, 1), video.at[:, height - 1], seen.at[new, top], vsems, 1),
        piece(0, -1, inside(0, -1), video.at[:, 0], seen.at[new, bottom], vsems, 2),
        piece(1, 1, inside(1, 1) & odd, video.at[last, height - 1], seen.at[old, top], vsems, 3),
        piece(1, -1, inside(1, -1) & odd, video.at[last, 0], seen.at[old, bottom], vsems, 4),
    ]
    for part in halo:
        start(part)
    even = jnp.logical_not(odd)
    newest = pl.ds(frames, 2)
    passed = [
        piece(1, 0, inside(1, -1) & even, seen.at[newest, top], seen.at[old, top], vsems, 3),
        piece(1, 0, inside(1, 1) & even, seen.at[newest, bottom], seen.at[old, bottom], vsems, 4),
    ]

    def spread(target, fr, ro, lines):
        flat = lines.reshape((-1,) + lines.shape[-2:])
        for c, piece in enumerate(along_width(flat, width)):
            target[fr, ro, :, c * chans:(c + 1) * chans] = piece.reshape(lines.shape)

    def patch(source, a, b):
        return source[a:a + frames, b:b + height].reshape(rows, 3 * chans)

    def forward(*at):
        lines = jnp.concatenate([patch(patches, a, b) for a, b in at], axis=1)
        mat = jnp.concatenate([taps[a * 3 + b] for a, b in at], axis=0)
        return jnp.dot(lines, mat, preferred_element_type=F32)

    loads[0].wait()
    spread(patches, new, own, seen[new, own])
    loads[1].wait()
    pre = forward((2, 1))
    arrive(halo[0], -1, 0, seen.at[old, own])
    spread(patches, old, own, seen[old, own])
    pre = pre + forward((0, 1), (1, 1))
    arrive(halo[1], 0, -1, seen.at[new, top])
    start(passed[0])
    arrive(halo[2], 0, 1, seen.at[new, bottom])
    start(passed[1])
    spread(patches, new, top, seen[new, top])
    spread(patches, new, bottom, seen[new, bottom])
    pre = pre + forward((2, 0), (2, 2))
    arrive(halo[3], -1, -1, seen.at[old, top])
    spread(patches, old, top, seen[old, top])
    arrive(halo[4], -1, 1, seen.at[old, bottom])
    spread(patches, old, bottom, seen[old, bottom])
    pre = pre + forward((0, 0), (1, 0), (0, 2), (1, 2))

    sig = 1.0 / (1.0 + jnp.exp(-pre))
    act[...] = (pre * sig).astype(BF16).reshape(act.shape)
    loads[2].wait()
    cot_flat = cot_own[...].reshape(rows, chans).astype(F32)
    grad = (cot_flat * sig * (1.0 + pre * (1.0 - sig))).astype(BF16)
    mine, later = pl.ds(0, frames), pl.ds(frames, 2)
    early = pl.ds(0, 2)
    gext[mine, own] = grad.reshape(video.shape)
    ghalo = [
        piece(-1, 0, inside(-1, 0), gext.at[early, own], gext.at[later, own], gsems, 0),
        piece(0, 1, inside(0, 1), gext.at[mine, height], gext.at[mine, top], gsems, 1),
        piece(0, -1, inside(0, -1), gext.at[mine, 1], gext.at[mine, bottom], gsems, 2),
        piece(-1, 0, inside(-1, -1), gext.at[early, top], gext.at[later, top], gsems, 3),
        piece(-1, 0, inside(-1, 1), gext.at[early, bottom], gext.at[later, bottom], gsems, 4),
    ]
    for part in ghalo[:3]:
        start(part)

    turned = grad.astype(F32).T.astype(BF16)
    kdepth = 3 * chans

    def weight_part(k):
        total[:, k * kdepth:(k + 1) * kdepth] = jnp.dot(
            turned, patch(patches, k // 3, k % 3), preferred_element_type=F32
        )

    def backward(a, b):
        block = taps.at[(2 - a) * 3 + 2 - b]
        mat = jnp.concatenate(
            [block[(2 - c) * chans:(3 - c) * chans, :] for c in range(3)], axis=1
        )
        return lax.dot_general(
            patch(gpatches, a, b), mat, (((1,), (1,)), ((), ())), preferred_element_type=F32
        )

    def grad_own():
        spread(gpatches, mine, own, grad.reshape(video.shape))
        return backward(0, 1)

    def grad_later(out):
        arrive(ghalo[0], 1, 0, gext.at[later, own])
        spread(gpatches, later, own, gext[later, own])
        return out + backward(1, 1) + backward(2, 1)

    def grad_rows():
        arrive(ghalo[1], 0, -1, gext.at[mine, top])
        start(ghalo[3])
        arrive(ghalo[2], 0, 1, gext.at[mine, bottom])
        start(ghalo[4])

    def grad_edges(out):
        for ro in (top, bottom):
            spread(gpatches, mine, ro, gext[mine, ro])
        return out + backward(0, 0) + backward(0, 2)

    def grad_corners(out):
        arrive(ghalo[3], 1, -1, gext.at[later, top])
        spread(gpatches, later, top, gext[later, top])
        out = out + backward(1, 0) + backward(2, 0)
        arrive(ghalo[4], 1, 1, gext.at[later, bottom])
        spread(gpatches, later, bottom, gext[later, bottom])
        out = out + backward(1, 2) + backward(2, 2)
        igrad[...] = out.astype(BF16).reshape(igrad.shape)

    def finish():
        for part in halo + passed + ghalo:
            sent(part)

    if not reduce_here:
        for k in range(9):
            weight_part(k)
        kgrad[...] = total[...]
        out = grad_later(grad_own())
        grad_rows()
        grad_corners(grad_edges(out))
        finish()
        return

    columns = total.shape[1] // nt
    wide = chunks.shape[-1]

    def cut(j):
        start = columns * j // 128 * 128
        shift = columns * j - start
        span = -(-(shift + columns) // 128) * 128
        piece = total[:, start:start + span]
        if shift:
            piece = pltpu.roll(piece, span - shift, 1)
        chunks[j] = piece[:, :wide].reshape(chunks.shape[1:])

    def send(k, source, target, device):
        copy = pltpu.make_async_remote_copy(
            src_ref=source, dst_ref=target,
            send_sem=ksend.at[k], recv_sem=krecv.at[k],
            device_id=device, device_id_type=MESH,
        )
        copy.start()
        return copy

    copies = []
    done = 0
    for half in range(2):
        need = -(-columns * (2 * half + 2) // kdepth)
        for k in range(done, need):
            weight_part(k)
        done = need
        cut(2 * half)
        cut(2 * half + 1)
        s0[half] = chunks[2 * half + 1 - core].astype(BF16)
        copies.append(send(half, s0.at[half], r0.at[half], other_core))

    out = grad_own()

    for half in range(2):
        copies[half].wait_recv()
        a1[half] = chunks[2 * half + core] + r0[half].astype(F32)
    s1a[...] = a1[1 - across, 0:2].astype(BF16)
    copies.append(send(2, s1a, r1a, other_across))
    s1b[...] = a1[:, 2:4, 1 - side].astype(BF16)
    copies.append(send(3, s1b, r1b, other_side))

    grad_rows()
    out = grad_later(out)

    copies[2].wait_recv()
    a2a[...] = a1[across, 0:2] + r1a[...].astype(F32)
    s2a[...] = a2a[:, 1 - side].astype(BF16)
    copies.append(send(4, s2a, r2a, other_side))
    copies[3].wait_recv()
    a2b[...] = a1[:, 2:4, side] + r1b[...].astype(F32)
    s2b[...] = a2b[1 - across].astype(BF16)
    copies.append(send(5, s2b, r2b, other_across))

    out = grad_edges(out)

    copies[4].wait_recv()
    a3[0:2] = a2a[:, side] + r2a[...].astype(F32)
    copies[5].wait_recv()
    a3[2:4] = a2b[across] + r2b[...].astype(F32)
    for k in (1, 2, 3):
        s3[k - 1] = a3[layers[k]].astype(BF16)
        copies.append(
            send(5 + k, s3.at[k - 1], r3.at[k - 1], (tm, layers[k] * 2 + side))
        )

    grad_corners(out)

    owned = a3[depth]
    for k in (1, 2, 3):
        copies[5 + k].wait_recv()
        owned = owned + r3[k - 1].astype(F32)
    kgrad[...] = owned[:, :columns]
    for copy in copies:
        copy.wait_send()
    finish()


def deliver(*refs):
    count = (len(refs) - 1) // 2
    copies = [pltpu.make_async_copy(refs[k], refs[count + k], refs[-1].at[k]) for k in range(count)]
    for copy in copies:
        copy.start()
    for copy in copies:
        copy.wait()


def local(nt, nr, video, weights, cotangent):
    frames, height, width, chans = video.shape
    rows = frames * height * width
    cols = 27 * chans
    share, columns = chans // nr, cols // nt
    reduce_here = nt == 4 and nr == 8 and share % 16 == 0
    wide = -(-columns // 128) * 128 if reduce_here else 128
    sh = share if reduce_here else 16
    vm = pltpu.VMEM
    far = pl.BlockSpec(memory_space=pl.ANY)
    kshape = (share, columns) if reduce_here else (chans, cols)
    scratch = [
        vm((9, 3 * chans, chans), BF16),
        vm(video.shape, BF16),
        vm((frames + 2, height + 2, width, chans), BF16),
        vm((frames + 2, height + 2, width, 3 * chans), BF16),
        vm((frames + 2, height + 2, width, chans), BF16),
        vm((frames + 2, height + 2, width, 3 * chans), BF16),
        vm((chans, cols), F32),
        vm((4, 4, 2, sh, wide), F32),
        vm((2, 4, 2, sh, wide), BF16),
        vm((2, 4, 2, sh, wide), BF16),
        vm((2, 4, 2, sh, wide), F32),
        vm((2, 2, sh, wide), BF16),
        vm((2, 2, sh, wide), BF16),
        vm((2, 2, sh, wide), BF16),
        vm((2, 2, sh, wide), BF16),
        vm((2, 2, sh, wide), F32),
        vm((2, 2, sh, wide), F32),
        vm((2, sh, wide), BF16),
        vm((2, sh, wide), BF16),
        vm((2, sh, wide), BF16),
        vm((2, sh, wide), BF16),
        vm((4, sh, wide), F32),
        vm((3, sh, wide), BF16),
        vm((3, sh, wide), BF16),
        pltpu.SemaphoreType.DMA((3,)),
        pltpu.SemaphoreType.DMA((5,)),
        pltpu.SemaphoreType.DMA((5,)),
        pltpu.SemaphoreType.DMA((5,)),
        pltpu.SemaphoreType.DMA((5,)),
        pltpu.SemaphoreType.DMA((9,)),
        pltpu.SemaphoreType.DMA((9,)),
    ]
    activated, input_grad, kgrad = pl.pallas_call(
        functools.partial(kernel, nt, nr, reduce_here),
        out_shape=(
            jax.ShapeDtypeStruct(video.shape, BF16),
            jax.ShapeDtypeStruct(video.shape, BF16),
            jax.ShapeDtypeStruct(kshape, F32),
        ),
        in_specs=[far, far, far],
        out_specs=(pl.BlockSpec(memory_space=pltpu.VMEM),) * 3,
        scratch_shapes=scratch,
        compiler_params=pltpu.CompilerParams(
            collective_id=0, has_side_effects=True, vmem_limit_bytes=VMEM_BYTES
        ),
        cost_estimate=pl.CostEstimate(
            flops=6 * rows * cols * chans, bytes_accessed=4 * 1024 * 1024, transcendentals=rows * chans
        ),
        name="conv_silu_grads",
    )(video, weights.reshape(9, 3 * chans, chans), cotangent)
    if not reduce_here:
        kgrad = lax.psum_scatter(kgrad, "rows", scatter_dimension=0, tiled=True)
        kgrad = lax.psum_scatter(kgrad, "tm", scatter_dimension=1, tiled=True)
        return activated, input_grad, kgrad
    results = (activated, input_grad, kgrad)
    return pl.pallas_call(
        deliver,
        out_shape=tuple(jax.ShapeDtypeStruct(x.shape, x.dtype) for x in results),
        in_specs=[pl.BlockSpec(memory_space=pltpu.VMEM)] * 3,
        out_specs=(far,) * 3,
        scratch_shapes=[pltpu.SemaphoreType.DMA((3,))],
        compiler_params=pltpu.CompilerParams(vmem_limit_bytes=4 * 1024 * 1024),
        name="deliver",
    )(*results)


def solution(mesh):
    split = P("tm", "rows", None, None)
    return jax.shard_map(
        functools.partial(local, mesh.shape["tm"], mesh.shape["rows"]),
        mesh=mesh,
        in_specs=(split, P(), split),
        out_specs=(split, split, P("rows", "tm")),
        check_vma=False,
    )
```
